32 devices in a mesh: dp: 8 (over z, y), head: 4 (over x, core).
Axes of the slice: x: 2, y: 2, z: 4, core: 2. Of those that a mesh axis runs over, the one named last changes fastest.
Arguments:
- tokens: bfloat16 [32768, 768], P(('dp', 'head')), may hold values from -6 to 6
- w_query: bfloat16 [768, 768], replicated, may hold values from -0.21875 to 0.21875
- w_key: bfloat16 [768, 768], replicated, may hold values from -0.21875 to 0.21875
- w_value: bfloat16 [768, 768], replicated, may hold values from -0.21875 to 0.21875
- w_out: bfloat16 [768, 768], replicated, may hold values from -6 to 6
- w_up: bfloat16 [768, 3072], replicated, may hold values from -0.21875 to 0.21875
- w_down: bfloat16 [3072, 768], replicated, may hold values from -0.109375 to 0.109375
- norm_gains: float32 [2, 768], replicated, may hold values from 0.25 to 1.75
- norm_biases: float32 [2, 768], replicated, may hold values from -2 to 2
- cotangent: bfloat16 [32768, 768], P(('dp', 'head')), may hold values from -6 to 6
Outputs:
- output: bfloat16 [32768, 768], P(('dp', 'head'))
- d_tokens: float32 [32768, 768], P(('dp', 'head'))
- grad_w_query: float32 [768, 768], replicated
- grad_w_key: float32 [768, 768], replicated
- grad_w_value: float32 [768, 768], replicated
- grad_w_out: float32 [768, 768], replicated
- grad_w_up: float32 [768, 3072], replicated
- grad_w_down: float32 [3072, 768], replicated
- grad_norm_gains: float32 [2, 768], replicated
- grad_norm_biases: float32 [2, 768], replicated
The draws below stay inside these ranges and needn't reach their ends.
All inputs are finite; a program needn't handle non-finite values.
Results may differ from the reference program's by a relative error of at most 0.014.
Values may be sent and summed in bfloat16 or wider, within the bound.
No kernel may reach another device: no remote copies, remote signals or barrier semaphores. Data moves between devices by JAX's collectives and lax.ppermute only.
A program may use at most 256 MiB of HBM per device.

```python
import math
import jax
import jax.numpy as jnp
from jax import lax

D = 768
H = 12
E = 64
FF = 3072
LENGTH = 2048
STRETCH = 128
SEQ_GROUP = 2
TOKENS = 32768
N_DP = 8


def level_of(rng, shape, shards, least, top_value):
    gain = 1.0
    for dim, parts in shards:
        heights = jax.random.uniform(jax.random.fold_in(jax.random.fold_in(rng, 6), dim), (parts,), jnp.float32, least / len(shards), top_value / len(shards))
        gain = gain * jnp.repeat(jnp.exp(heights), shape[dim] // parts).reshape((-1,) + (1,) * (len(shape) - 1 - dim))
    return gain


def noise(stream_key, extent, scale, reach, shards=(), held_as=jnp.bfloat16):
    gain = level_of(stream_key, extent, shards, -0.22, 0.18) if shards else 1.0
    drawn = jax.random.normal(stream_key, extent, jnp.float32) * scale * gain
    return jnp.minimum(jnp.maximum(drawn, -reach), reach).astype(held_as)


def setup_inputs(seed: int = 0) -> dict:
    key_of = jax.random.split(jax.random.key(seed), 11)
    return {
        "tokens": noise(key_of[0], (TOKENS, D), 1.0, 6.0, ((0, 32),)),
        "w_query": noise(key_of[1], (D, D), D ** -0.5, 0.21875),
        "w_key": noise(key_of[2], (D, D), D ** -0.5, 0.21875),
        "w_value": noise(key_of[3], (D, D), D ** -0.5, 0.21875),
        "w_out": noise(key_of[4], (D, D), (D * 2 // LENGTH + 1) ** -0.5, 6.0),
        "w_up": noise(key_of[5], (D, FF), D ** -0.5, 0.21875),
        "w_down": noise(key_of[6], (FF, D), FF ** -0.5, 0.109375),
        "norm_gains": jnp.clip(1.0 + 0.15 * jax.random.normal(key_of[7], (2, D), jnp.float32), 0.25, 1.75),
        "norm_biases": noise(key_of[8], (2, D), 0.3, 2.0, (), jnp.float32),
        "cotangent": noise(key_of[9], (TOKENS, D), 1.0, 6.0, ((0, 32),)),
    }


@jax.custom_vjp
def low(v):
    return lax.optimization_barrier(v.astype(jnp.bfloat16)).astype(jnp.float32)

@jax.custom_vjp
def low_back(v):
    return v

def low_keep(v):
    return (low(v), None)

def low_pass(kept, grad):
    return (grad,)

def back_keep(v):
    return (v, None)

def back_low(kept, grad):
    return (low(grad),)
low.defvjp(low_keep, low_pass)
low_back.defvjp(back_keep, back_low)
EPSILON = 1e-05
HIGHEST = lax.Precision.HIGHEST

def matmul_high(first_arg, second_arg):
    return jnp.dot(first_arg, second_arg, precision=HIGHEST, preferred_element_type=jnp.float32)

def layer_norm(inputs, norm_gain, norm_shift):
    centre = lax.optimization_barrier(jnp.mean(inputs, axis=-1, keepdims=True))
    centred = inputs - centre
    spread = lax.optimization_barrier(jnp.mean(centred * centred, axis=-1, keepdims=True))
    return centred * lax.rsqrt(spread + EPSILON) * norm_gain + norm_shift

def earlier_sum(blocks):
    running = jnp.cumsum(blocks, axis=1)
    return jnp.concatenate([jnp.zeros_like(running[:, :1]), running[:, :-1]], axis=1)

def cos_attention(queries, key_part, value_part):
    seq_count, seq_len, head_count, head_size = queries.shape
    block_count = seq_len // STRETCH
    step_angle = 0.5 * math.pi / seq_len
    angles = step_angle * jnp.arange(seq_len, dtype=jnp.float32)
    cosine = jnp.cos(angles)[None, :, None, None]
    sine_row = jnp.sin(angles)[None, :, None, None]
    blocked = (seq_count, block_count, STRETCH, head_count, head_size)
    q_block = queries.reshape(blocked)
    k_block = key_part.reshape(blocked)
    v_block = value_part.reshape(blocked)
    q_cos = (queries * cosine).reshape(blocked)
    q_sin = (queries * sine_row).reshape(blocked)
    k_cos = (key_part * cosine).reshape(blocked)
    k_sin = (key_part * sine_row).reshape(blocked)
    offsets = jnp.arange(STRETCH)
    distance = offsets[:, None] - offsets[None, :]
    weight_table = jnp.where(distance >= 0, jnp.cos(step_angle * distance.astype(jnp.float32)), 0.0)
    scores = jnp.einsum('sbihe,sbjhe->sbhij', q_block, k_block, precision=HIGHEST) * weight_table
    numerator = jnp.einsum('sbhij,sbjhe->sbihe', scores, v_block, precision=HIGHEST)
    denominator = jnp.einsum('sbhij->sbih', scores)
    state_cos = jnp.einsum('sbjhe,sbjhf->sbhef', k_cos, v_block, precision=HIGHEST)
    state_sin = jnp.einsum('sbjhe,sbjhf->sbhef', k_sin, v_block, precision=HIGHEST)
    total_cos = lax.optimization_barrier(jnp.sum(k_cos, axis=2))
    total_sin = lax.optimization_barrier(jnp.sum(k_sin, axis=2))
    numerator = numerator + jnp.einsum('sbihe,sbhef->sbihf', q_cos, earlier_sum(state_cos), precision=HIGHEST)
    numerator = numerator + jnp.einsum('sbihe,sbhef->sbihf', q_sin, earlier_sum(state_sin), precision=HIGHEST)
    denominator = denominator + jnp.einsum('sbihe,sbhe->sbih', q_cos, earlier_sum(total_cos), precision=HIGHEST)
    denominator = denominator + jnp.einsum('sbihe,sbhe->sbih', q_sin, earlier_sum(total_sin), precision=HIGHEST)
    return (numerator / denominator[..., None]).reshape(seq_count, seq_len, head_count, head_size)

def forward(inputs, w_query, w_key, w_value, w_out, w_up, w_down, norm_gains, norm_biases):
    token_count = inputs.shape[0]
    head_shape = (token_count // LENGTH, LENGTH, H, E)
    query_pre = low_back(matmul_high(inputs, w_query))
    key_pre = low_back(matmul_high(inputs, w_key))
    queries = low_back(low(jax.nn.softplus(query_pre)))
    key_low = low_back(low(jax.nn.softplus(key_pre)))
    value_low = low_back(low(matmul_high(inputs, w_value)))
    attended = cos_attention(queries.reshape(head_shape), key_low.reshape(head_shape), value_low.reshape(head_shape))
    mixed_low = low_back(low(attended.reshape(token_count, D)))
    branch = low_back(matmul_high(mixed_low, w_out))
    normed = layer_norm(inputs + branch, norm_gains[0], norm_biases[0])
    hidden_in = low_back(matmul_high(low(normed), w_up))
    hidden = low(jax.nn.gelu(hidden_in, approximate=False))
    ffn_out = low_back(matmul_high(hidden, w_down))
    return layer_norm(normed + ffn_out, norm_gains[1], norm_biases[1])

def reference(tokens, w_query, w_key, w_value, w_out, w_up, w_down, norm_gains, norm_biases, cotangent):
    params = (w_query.astype(jnp.float32), w_key.astype(jnp.float32), w_value.astype(jnp.float32), w_out.astype(jnp.float32), w_up.astype(jnp.float32), w_down.astype(jnp.float32), norm_gains, norm_biases)
    group_rows = SEQ_GROUP * LENGTH
    input_groups = tokens.astype(jnp.float32).reshape(N_DP, group_rows, D)
    grad_groups = cotangent.astype(jnp.float32).reshape(N_DP, group_rows, D)

    def one_group(totals, group_pair):
        result, pullback = jax.vjp(forward, group_pair[0], *params)
        gradients = pullback(group_pair[1])
        summed = tuple((running + gradient for running, gradient in zip(totals, gradients[1:])))
        return (summed, (result.astype(jnp.bfloat16), gradients[0]))
    initial = tuple((jnp.zeros_like(weight_arg) for weight_arg in params))
    totals, (outputs, d_groups) = lax.scan(one_group, initial, (input_groups, grad_groups))
    return (outputs.reshape(TOKENS, D), d_groups.reshape(TOKENS, D), totals[0], totals[1], totals[2], totals[3], totals[4], totals[5], totals[6], totals[7])
```

```python
import functools
import math

import jax
import jax.numpy as jnp
import numpy as np
from jax import lax
from jax.experimental import pallas as pl
from jax.experimental.pallas import tpu as pltpu
from jax.sharding import PartitionSpec as P

D = 768
E = 64
FF = 3072
LENGTH = 2048
CHUNK = 256
PAIR = 2 * E
PAIRS = D // PAIR
FEAT = 2 * PAIR
EPSILON = 1e-05
STEP_ANGLE = 0.5 * math.pi / LENGTH
QUARTER = D // 4
LIMIT = 56 * 2**20

f32 = jnp.float32
bf16 = jnp.bfloat16


def nn(a, b):
    return jnp.dot(a, b, preferred_element_type=f32)


def tn(a, b):
    return lax.dot_general(a, b, (((0,), (0,)), ((), ())), preferred_element_type=f32)


def nt(a, b):
    return lax.dot_general(a, b, (((1,), (1,)), ((), ())), preferred_element_type=f32)


def params(**kw):
    return pltpu.CompilerParams(vmem_limit_bytes=LIMIT, **kw)


def softplus(x):
    return jnp.maximum(x, 0.0) + jnp.log1p(jnp.exp(-jnp.abs(x)))


def lane_head(rows):
    return (lax.broadcasted_iota(jnp.int32, (rows, PAIR), 1) >= E).astype(jnp.int32)


def row_head():
    return (lax.broadcasted_iota(jnp.int32, (FEAT, PAIR), 0) % PAIR >= E).astype(jnp.int32)


def unpack_state(packed):
    same = row_head() == lane_head(FEAT)
    left = jnp.where(same, packed, 0.0)
    right = jnp.where(same, pltpu.roll(packed, E, 1), 0.0)
    return jnp.concatenate([left, right], axis=1).astype(bf16)


def features(x, cosine, sine):
    return jnp.concatenate([x * cosine, x * sine], axis=1).astype(bf16)


def with_ones(v):
    return jnp.concatenate([v, jnp.ones_like(v)], axis=1)


def project_kernel(tok, wq, wk, wv, cos, sin, q_ref, k_ref, v_ref, pre_ref, tot_ref):
    @pl.when(pl.program_id(0) == 0)
    def _():
        tot_ref[...] = jnp.zeros_like(tot_ref)

    x = tok[...]
    q_ref[...] = softplus(nn(x, wq[...])).astype(bf16)
    k = softplus(nn(x, wk[...])).astype(bf16)
    k_ref[...] = k
    v = nn(x, wv[...]).astype(bf16)
    v_ref[...] = v
    same = row_head() == lane_head(FEAT)
    for p in range(PAIRS):
        cols = slice(p * PAIR, (p + 1) * PAIR)
        k_feat = features(k[:, cols].astype(f32), cos[...], sin[...])
        both = tn(k_feat, with_ones(v[:, cols]))
        pre_ref[0, p] = tot_ref[p]
        tot_ref[p] += jnp.where(same, both[:, :PAIR], both[:, PAIR:])


def project(tokens, wq, wk, wv, cos, sin):
    rows = tokens.shape[0]
    steps = rows // CHUNK
    chunk = pl.BlockSpec((CHUNK, D), lambda i: (i, 0))
    weight = pl.BlockSpec((D, D), lambda i: (0, 0))
    table = pl.BlockSpec((CHUNK, PAIR), lambda i: (i, 0))
    act = jax.ShapeDtypeStruct((rows, D), bf16)
    return pl.pallas_call(
        project_kernel,
        grid=(steps,),
        in_specs=[chunk, weight, weight, weight, table, table],
        out_specs=[
            chunk,
            chunk,
            chunk,
            pl.BlockSpec((1, PAIRS, FEAT, PAIR), lambda i: (i, 0, 0, 0)),
            pl.BlockSpec((PAIRS, FEAT, PAIR), lambda i: (0, 0, 0)),
        ],
        out_shape=[
            act,
            act,
            act,
            jax.ShapeDtypeStruct((steps, PAIRS, FEAT, PAIR), f32),
            jax.ShapeDtypeStruct((PAIRS, FEAT, PAIR), f32),
        ],
        compiler_params=params(),
        cost_estimate=pl.CostEstimate(flops=6 * rows * D * D, bytes_accessed=16 * rows * D, transcendentals=0),
        name="project",
    )(tokens, wq, wk, wv, cos, sin)


def norm_parts(z):
    centred = z - jnp.mean(z, axis=-1, keepdims=True)
    rstd = lax.rsqrt(jnp.mean(centred * centred, axis=-1, keepdims=True) + EPSILON)
    return centred * rstd, rstd


def norm_back(t, n, rstd):
    return (t - jnp.mean(t, axis=-1, keepdims=True) - n * jnp.mean(t * n, axis=-1, keepdims=True)) * rstd


def forward_kernel(
    coef, tok, q_ref, k_ref, v_ref, pre, init, cos, sin, table, w_out, w_up, w_down, gains, biases, cot,
    mixed_ref, inv_ref, state_ref, n0_ref, rstd_ref, low_ref, hidden_ref, slope_ref, out_ref, dres_ref, dffn_ref, ng_ref,
):
    turn_cos, turn_sin = coef[0], coef[1]
    second = lane_head(CHUNK) == 1
    second2 = jnp.concatenate([second, second], axis=1)
    for p in range(PAIRS):
        cols = slice(p * PAIR, (p + 1) * PAIR)
        start_cos, start_sin = init[p, :PAIR], init[p, PAIR:]
        turned = jnp.concatenate(
            [turn_cos * start_cos + turn_sin * start_sin, turn_cos * start_sin - turn_sin * start_cos], axis=0
        )
        state = unpack_state(pre[0, p] + turned)
        state_ref[0, p] = state
        q, k, v = q_ref[:, cols], k_ref[:, cols], v_ref[:, cols]
        total = nn(features(q.astype(f32), cos[...], sin[...]), state)
        v_ones = with_ones(v)
        zero = jnp.zeros_like(q)
        score_0 = (nt(jnp.where(second, zero, q), k) * table[...]).astype(bf16)
        score_1 = (nt(jnp.where(second, q, zero), k) * table[...]).astype(bf16)
        total += jnp.where(second2, nn(score_1, v_ones), nn(score_0, v_ones))
        inv = 1.0 / total[:, PAIR:]
        mixed_ref[:, cols] = (total[:, :PAIR] * inv).astype(bf16)
        inv_ref[:, cols] = inv
    z = tok[...].astype(f32) + nn(mixed_ref[...], w_out[...])
    n0, rstd = norm_parts(z)
    n0_ref[...] = n0.astype(bf16)
    rstd_ref[...] = jnp.broadcast_to(rstd, rstd_ref.shape)
    normed = n0 * gains[0:1] + biases[0:1]
    low = normed.astype(bf16)
    low_ref[...] = low
    for j in range(FF // D):
        cols = slice(j * D, (j + 1) * D)
        h = nn(low, w_up[:, cols])
        phi = 0.5 * (1.0 + lax.erf(h * (0.5**0.5)))
        hidden_ref[:, cols] = (h * phi).astype(bf16)
        slope_ref[:, cols] = (phi + h * jnp.exp(-0.5 * h * h) * ((2 * math.pi) ** -0.5)).astype(bf16)
    z = normed + nn(hidden_ref[...], w_down[...])
    n1, rstd = norm_parts(z)
    out_ref[...] = (n1 * gains[1:2] + biases[1:2]).astype(bf16)
    g = cot[...].astype(f32)
    dres = norm_back(g * gains[1:2], n1, rstd)
    dres_ref[...] = dres
    dffn_ref[...] = dres.astype(bf16)

    @pl.when(pl.program_id(0) == 0)
    def _():
        ng_ref[...] = jnp.zeros_like(ng_ref)

    ng_ref[0:1] += jnp.sum(g * n1, axis=0, keepdims=True)
    ng_ref[1:2] += jnp.sum(g, axis=0, keepdims=True)


def forward(coef, tokens, q, k, v, pre, init, cos, sin, table, w_out, w_up, w_down, gains, biases, cot):
    rows = tokens.shape[0]
    steps = rows // CHUNK
    chunk = pl.BlockSpec((CHUNK, D), lambda i: (i, 0))
    wide = pl.BlockSpec((CHUNK, FF), lambda i: (i, 0))
    thin = pl.BlockSpec((CHUNK, PAIR), lambda i: (i, 0))

    def whole(*shape):
        return pl.BlockSpec(shape, lambda i: (0,) * len(shape))

    state = pl.BlockSpec((1, PAIRS, FEAT, PAIR), lambda i: (i, 0, 0, 0))
    state_out = pl.BlockSpec((1, PAIRS, FEAT, FEAT), lambda i: (i, 0, 0, 0))

    def make(width, dtype):
        return jax.ShapeDtypeStruct((rows, width), dtype)

    return pl.pallas_call(
        forward_kernel,
        grid=(steps,),
        in_specs=[
            pl.BlockSpec(memory_space=pltpu.SMEM), chunk, chunk, chunk, chunk, state, whole(PAIRS, FEAT, PAIR), thin, thin,
            whole(CHUNK, CHUNK), whole(D, D), whole(D, FF), whole(FF, D), whole(2, D), whole(2, D), chunk,
        ],
        out_specs=[chunk, chunk, state_out, chunk, thin, chunk, wide, wide, chunk, chunk, chunk, whole(2, D)],
        out_shape=[
            make(D, bf16), make(D, f32), jax.ShapeDtypeStruct((steps, PAIRS, FEAT, FEAT), bf16), make(D, bf16),
            make(PAIR, f32), make(D, bf16), make(FF, bf16), make(FF, bf16), make(D, bf16), make(D, f32), make(D, bf16),
            jax.ShapeDtypeStruct((2, D), f32),
        ],
        compiler_params=params(),
        cost_estimate=pl.CostEstimate(
            flops=2 * rows * (D * D + 2 * D * FF) + 24 * 6 * 2 * 256**3, bytes_accessed=60 * rows * D, transcendentals=0
        ),
        name="forward",
    )(coef, tokens, q, k, v, pre, init, cos, sin, table, w_out, w_up, w_down, gains, biases, cot)


def backward_kernel(
    dffn, slope, dres, n0_ref, rstd_ref, mixed, inv, q_ref, cos, sin, w_out, w_up, w_down, gains,
    dhid_ref, dres_one_ref, dbranch_ref, dnum_ref, dden_ref, part_ref, tot_ref, ng_ref,
):
    @pl.when(pl.program_id(0) == 0)
    def _():
        ng_ref[...] = jnp.zeros_like(ng_ref)
        tot_ref[...] = jnp.zeros_like(tot_ref)

    for j in range(FF // D):
        cols = slice(j * D, (j + 1) * D)
        dhid_ref[:, cols] = (nt(dffn[...], w_down[cols, :]) * slope[:, cols].astype(f32)).astype(bf16)
    g = dres[...] + nt(dhid_ref[...], w_up[...])
    n0 = n0_ref[...].astype(f32)
    ng_ref[0:1] += jnp.sum(g * n0, axis=0, keepdims=True)
    ng_ref[1:2] += jnp.sum(g, axis=0, keepdims=True)
    dres_one = norm_back(g * gains[0:1], n0, rstd_ref[:, 0:1])
    dres_one_ref[...] = dres_one
    dbranch = dres_one.astype(bf16)
    dbranch_ref[...] = dbranch
    dmixed = nt(dbranch, w_out[...]).astype(bf16).astype(f32)
    second = lane_head(CHUNK) == 1
    lane = lax.broadcasted_iota(jnp.int32, (CHUNK, PAIR), 1)
    same = row_head() == lane_head(FEAT)
    for p in range(PAIRS):
        cols = slice(p * PAIR, (p + 1) * PAIR)
        inv_p = inv[:, cols]
        dnum = (dmixed[:, cols] * inv_p).astype(bf16)
        dnum_ref[:, cols] = dnum
        moment = dnum.astype(f32) * mixed[:, cols].astype(f32)
        first_sum = jnp.sum(jnp.where(second, 0.0, moment), axis=1, keepdims=True)
        second_sum = jnp.sum(jnp.where(second, moment, 0.0), axis=1, keepdims=True)
        dden = jnp.where(second, second_sum, first_sum) * (-2.0 / E)
        high = dden.astype(bf16)
        rest = (dden - high.astype(f32)).astype(bf16)
        dden = jnp.where(lane % E < E // 2, high, rest)
        dden_ref[:, cols] = dden
        both = tn(features(q_ref[:, cols].astype(f32), cos[...], sin[...]), jnp.concatenate([dnum, dden], axis=1))
        part = jnp.where(same, both[:, :PAIR], pltpu.roll(both[:, PAIR:], E, 1))
        part_ref[0, p] = part
        tot_ref[p] += part


def backward(dffn, slope, dres, n0, rstd, mixed, inv, q, cos, sin, w_out, w_up, w_down, gains):
    rows = dffn.shape[0]
    steps = rows // CHUNK
    chunk = pl.BlockSpec((CHUNK, D), lambda i: (i, 0))
    wide = pl.BlockSpec((CHUNK, FF), lambda i: (i, 0))
    thin = pl.BlockSpec((CHUNK, PAIR), lambda i: (i, 0))

    def whole(*shape):
        return pl.BlockSpec(shape, lambda i: (0,) * len(shape))

    def make(width, dtype):
        return jax.ShapeDtypeStruct((rows, width), dtype)

    return pl.pallas_call(
        backward_kernel,
        grid=(steps,),
        in_specs=[
            chunk, wide, chunk, chunk, thin, chunk, chunk, chunk, thin, thin,
            whole(D, D), whole(D, FF), whole(FF, D), whole(2, D),
        ],
        out_specs=[
            wide, chunk, chunk, chunk, chunk, pl.BlockSpec((1, PAIRS, FEAT, PAIR), lambda i: (i, 0, 0, 0)),
            whole(PAIRS, FEAT, PAIR), whole(2, D),
        ],
        out_shape=[
            make(FF, bf16), make(D, f32), make(D, bf16), make(D, bf16), make(D, bf16),
            jax.ShapeDtypeStruct((steps, PAIRS, FEAT, PAIR), f32), jax.ShapeDtypeStruct((PAIRS, FEAT, PAIR), f32),
            jax.ShapeDtypeStruct((2, D), f32),
        ],
        compiler_params=params(),
        cost_estimate=pl.CostEstimate(
            flops=2 * rows * (D * D + 2 * D * FF), bytes_accessed=50 * rows * D, transcendentals=0
        ),
        name="backward",
    )(dffn, slope, dres, n0, rstd, mixed, inv, q, cos, sin, w_out, w_up, w_down, gains)


def attend_back_kernel(
    coef, q_ref, k_ref, v_ref, dnum_ref, dden_ref, state_ref, part, init, cos, sin, table, table_t,
    dq_ref, dk_ref, dv_ref, run,
):
    @pl.when(pl.program_id(0) == 0)
    def _():
        turn_cos, turn_sin = coef[0], coef[1]
        for p in range(PAIRS):
            d_cos, d_sin = init[p, :PAIR], init[p, PAIR:]
            run[p, :PAIR] = turn_cos * d_cos - turn_sin * d_sin
            run[p, PAIR:] = turn_sin * d_cos + turn_cos * d_sin

    second = lane_head(CHUNK) == 1
    second2 = jnp.concatenate([second, second], axis=1)

    def split(x, mask):
        zero = jnp.zeros_like(x)
        return jnp.where(mask, zero, x), jnp.where(mask, x, zero)

    for p in range(PAIRS):
        cols = slice(p * PAIR, (p + 1) * PAIR)
        q, k, v = q_ref[:, cols], k_ref[:, cols], v_ref[:, cols]
        q_wide, k_wide = q.astype(f32), k.astype(f32)
        dnum = dnum_ref[:, cols]
        grad = jnp.concatenate([dnum, dden_ref[:, cols]], axis=1)
        v_ones = with_ones(v)
        d_state = unpack_state(run[p])
        run[p] += part[0, p]
        dq_feat = nt(grad, state_ref[0, p])
        dk_feat = nt(v_ones, d_state)
        dv = nn(features(k_wide, cos[...], sin[...]), d_state[:, :PAIR])
        dq = dq_feat[:, :PAIR] * cos[...] + dq_feat[:, PAIR:] * sin[...]
        dk = dk_feat[:, :PAIR] * cos[...] + dk_feat[:, PAIR:] * sin[...]
        for grad_h, q_h, k_h, dnum_h in zip(split(grad, second2), split(q, second), split(k, second), split(dnum, second)):
            d_score = (nt(grad_h, v_ones) * table[...]).astype(bf16)
            dq += nn(d_score, k_h)
            score_t = (nt(k_h, q) * table_t[...]).astype(bf16)
            d_score_t = (nt(v_ones, grad_h) * table_t[...]).astype(bf16)
            dk += nn(d_score_t, q_h)
            dv += nn(score_t, dnum_h)
        dq_ref[:, cols] = (dq.astype(bf16).astype(f32) * sigmoid_of(q_wide)).astype(bf16)
        dk_ref[:, cols] = (dk.astype(bf16).astype(f32) * sigmoid_of(k_wide)).astype(bf16)
        dv_ref[:, cols] = dv.astype(bf16)


def sigmoid_of(soft):
    return jnp.where(soft < 0.01, soft * (1.0 - 0.5 * soft), 1.0 - jnp.exp(-soft))


def attend_back(coef, q, k, v, dnum, dden, state, part, init, cos, sin, table, table_t):
    rows = q.shape[0]
    steps = rows // CHUNK
    last = steps - 1
    chunk = pl.BlockSpec((CHUNK, D), lambda i: (last - i, 0))
    thin = pl.BlockSpec((CHUNK, PAIR), lambda i: (last - i, 0))
    square = pl.BlockSpec((CHUNK, CHUNK), lambda i: (0, 0))
    act = jax.ShapeDtypeStruct((rows, D), bf16)
    return pl.pallas_call(
        attend_back_kernel,
        grid=(steps,),
        in_specs=[
            pl.BlockSpec(memory_space=pltpu.SMEM), chunk, chunk, chunk, chunk, chunk,
            pl.BlockSpec((1, PAIRS, FEAT, FEAT), lambda i: (last - i, 0, 0, 0)),
            pl.BlockSpec((1, PAIRS, FEAT, PAIR), lambda i: (last - i, 0, 0, 0)),
            pl.BlockSpec((PAIRS, FEAT, PAIR), lambda i: (0, 0, 0)), thin, thin, square, square,
        ],
        out_specs=[chunk, chunk, chunk],
        out_shape=[act, act, act],
        scratch_shapes=[pltpu.VMEM((PAIRS, FEAT, PAIR), f32)],
        compiler_params=params(),
        cost_estimate=pl.CostEstimate(flops=24 * 16 * 2 * 256**3, bytes_accessed=24 * rows * D, transcendentals=0),
        name="attend_back",
    )(coef, q, k, v, dnum, dden, state, part, init, cos, sin, table, table_t)


def token_grad_kernel(dres_one, dq, dk, dv, wq, wk, wv, out):
    out[...] = dres_one[...] + nt(dq[...], wq[...]) + nt(dk[...], wk[...]) + nt(dv[...], wv[...])


def token_grad(dres_one, dq, dk, dv, wq, wk, wv):
    rows = dq.shape[0]
    chunk = pl.BlockSpec((CHUNK, D), lambda i: (i, 0))
    weight = pl.BlockSpec((D, D), lambda i: (0, 0))
    return pl.pallas_call(
        token_grad_kernel,
        grid=(rows // CHUNK,),
        in_specs=[chunk] * 4 + [weight] * 3,
        out_specs=chunk,
        out_shape=jax.ShapeDtypeStruct((rows, D), f32),
        compiler_params=params(),
        cost_estimate=pl.CostEstimate(flops=6 * rows * D * D, bytes_accessed=14 * rows * D, transcendentals=0),
        name="token_grad",
    )(dres_one, dq, dk, dv, wq, wk, wv)


def place_rows(value, ref, me, block, index):
    for b in range(D // block):
        to = pl.multiple_of((jnp.int32(b) ^ me) * block, block)
        ref[index, pl.ds(to, block), :] = value[b * block : (b + 1) * block]


def unit_send_kernel(block, pick, sc, a, b, out):
    u = pl.program_id(0)
    place_rows(tn(a[...], b[...]).astype(bf16), out, sc[1 + u], block, 0)


def unit_keep_kernel(block, pick, sc, a, b, got, out, wide):
    u = pl.program_id(0)
    place_rows(tn(a[...], b[...]), wide, sc[1 + u], block, 0)
    out[0] = (wide[0] + got[0].astype(f32)).astype(bf16)


def unit_call(sc, a, b, own, block, a_split, b_split, got=None):
    rows = a.shape[0]

    def unit(i, sc):
        return 2 * (sc[0] if own else 1 - sc[0]) + i

    def spec(split):
        return pl.BlockSpec((rows, D), (lambda i, sc: (0, unit(i, sc))) if split else (lambda i, sc: (0, 0)))

    out_spec = pl.BlockSpec((1, D, D), lambda i, sc: (i, 0, 0))
    ins, specs, scratch = [a, b], [spec(a_split), spec(b_split)], []
    kernel = unit_send_kernel
    if got is not None:
        ins.append(got)
        specs.append(out_spec)
        scratch = [pltpu.VMEM((1, D, D), f32)]
        kernel = unit_keep_kernel
    return pl.pallas_call(
        functools.partial(kernel, block, None),
        grid_spec=pltpu.PrefetchScalarGridSpec(
            num_scalar_prefetch=1, grid=(2,), in_specs=specs, out_specs=out_spec, scratch_shapes=scratch
        ),
        out_shape=jax.ShapeDtypeStruct((2, D, D), bf16),
        compiler_params=params(),
        cost_estimate=pl.CostEstimate(flops=4 * rows * D * D, bytes_accessed=8 * rows * D, transcendentals=0),
        name="unit_keep" if own else "unit_send",
    )(sc, *ins)


def pick_kernel(block, unit, sc, mine, other, out):
    owner, me = unit // 2, sc[1 + unit % 2]

    def put(ref):
        for b in range(D // block):
            at = pl.multiple_of((jnp.int32(b) ^ me) * block, block)
            out[b * block : (b + 1) * block, :] = ref[0, pl.ds(at, block), :].astype(f32)

    @pl.when(sc[0] == owner)
    def _():
        put(mine)

    @pl.when(sc[0] != owner)
    def _():
        put(other)


def pick_unit(sc, mine, other, unit, block):
    spec = pl.BlockSpec((1, D, D), lambda i, sc: (unit % 2, 0, 0))
    return pl.pallas_call(
        functools.partial(pick_kernel, block, unit),
        grid_spec=pltpu.PrefetchScalarGridSpec(
            num_scalar_prefetch=1,
            grid=(1,),
            in_specs=[spec, spec],
            out_specs=pl.BlockSpec((D, D), lambda i, sc: (0, 0)),
        ),
        out_shape=jax.ShapeDtypeStruct((D, D), f32),
        compiler_params=params(),
        name="pick_unit",
    )(sc, mine, other)


def gather_kernel(block, sc, mine, other, out):
    g = pl.program_id(0)
    me = jnp.where(g % 2 == 0, sc[1], sc[2])

    def put(ref):
        for b in range(D // block):
            at = pl.multiple_of((jnp.int32(b) ^ me) * block, block)
            out[b * block : (b + 1) * block, :] = ref[0, pl.ds(at, block), :].astype(f32)

    @pl.when(g // 2 == sc[0])
    def _():
        put(mine)

    @pl.when(g // 2 != sc[0])
    def _():
        put(other)


def gather_units(sc, mine, other, block, by_rows):
    def at(own):
        def index(g, sc):
            first = 2 * (sc[0] if own else 1 - sc[0])
            return (jnp.clip(g - first, 0, 1), 0, 0)

        return index

    return pl.pallas_call(
        functools.partial(gather_kernel, block),
        grid_spec=pltpu.PrefetchScalarGridSpec(
            num_scalar_prefetch=1,
            grid=(4,),
            in_specs=[pl.BlockSpec((1, D, D), at(True)), pl.BlockSpec((1, D, D), at(False))],
            out_specs=pl.BlockSpec((D, D), (lambda g, sc: (g, 0)) if by_rows else (lambda g, sc: (0, g))),
        ),
        out_shape=jax.ShapeDtypeStruct((4 * D, D) if by_rows else (D, 4 * D), f32),
        compiler_params=params(),
        name="gather_units",
    )(sc, mine, other)


def add_low(*terms):
    total = terms[0].astype(f32)
    for term in terms[1:]:
        total = total + term.astype(f32)
    return total.astype(bf16)


def make_local(n_dp, n_head):
    n_z = n_dp // 2
    direct = QUARTER % (16 * n_z) == 0 and n_z & (n_z - 1) == 0
    places = n_z if direct else 1
    block = QUARTER // places

    def swap(x, axis, size, bit):
        return lax.ppermute(x, axis, [(i, i ^ bit) for i in range(size)])

    def swap_core(x):
        return swap(x, "head", n_head, 1)

    def swap_x(x):
        return swap(x, "head", n_head, 2)

    def swap_y(x):
        return swap(x, "dp", n_dp, 1)

    def swap_z(x, k):
        return swap(x, "dp", n_dp, 2 * k)

    half = D // 2

    def reduce_units(units):
        a, b = units[0], units[1]
        got_a, got_b = swap_x(a[half:]), swap_y(b[half:])
        a, b = add_low(a[:half], got_a), add_low(b[:half], got_b)
        got_a, got_b = swap_y(a[QUARTER:]), swap_x(b[QUARTER:])
        if direct:
            def part(k):
                at = slice(k * block, (k + 1) * block)
                return jnp.concatenate([add_low(a[at], got_a[at]), add_low(b[at], got_b[at])])

            got = [swap_z(part(k), k) for k in range(1, n_z)]
            share = add_low(part(0), *got)
            parts = [share] + [swap_z(share, k) for k in range(1, n_z)]
            a = jnp.concatenate([p[:block] for p in parts])
            b = jnp.concatenate([p[block:] for p in parts])
        else:
            both = jnp.concatenate([add_low(a[:QUARTER], got_a), add_low(b[:QUARTER], got_b)])
            same_z = [[2 * z + y for z in range(n_z)] for y in range(2)]
            both = lax.psum(both.astype(f32), "dp", axis_index_groups=same_z).astype(bf16)
            a, b = both[:QUARTER], both[QUARTER:]
        got_a, got_b = swap_y(a), swap_x(b)
        a, b = jnp.concatenate([a, got_a]), jnp.concatenate([b, got_b])
        got_a, got_b = swap_x(a), swap_y(b)
        return jnp.stack([jnp.concatenate([a, got_a]), jnp.concatenate([b, got_b])])

    def local(tokens, w_query, w_key, w_value, w_out, w_up, w_down, norm_gains, norm_biases, cotangent):
        rows = tokens.shape[0]
        assert LENGTH == 2 * rows and n_head % 4 == 0 and n_dp % 2 == 0
        head, dp = lax.axis_index("head"), lax.axis_index("dp")
        core, x, y, z = head % 2, head // 2, dp % 2, dp // 2
        rank = z if direct else 0
        sc = jnp.stack([core, (2 * x + y) * places + rank, (2 * y + x) * places + rank]).astype(jnp.int32)
        angle = STEP_ANGLE * np.arange(rows)
        cos = jnp.asarray(np.broadcast_to(np.cos(angle)[:, None], (rows, PAIR)), f32)
        sin = jnp.asarray(np.broadcast_to(np.sin(angle)[:, None], (rows, PAIR)), f32)
        gap = np.arange(CHUNK)[:, None] - np.arange(CHUNK)[None, :]
        weights = np.where(gap >= 0, np.cos(STEP_ANGLE * gap), 0.0)
        table, table_t = jnp.asarray(weights, f32), jnp.asarray(weights.T, f32)
        turn = jnp.asarray([math.cos(STEP_ANGLE * rows), math.sin(STEP_ANGLE * rows)], f32)
        later = core.astype(f32)

        q, k, v, pre, total = project(tokens, w_query, w_key, w_value, cos, sin)
        init = swap_core(total)
        mixed, inv, state, n0, rstd, low, hidden, slope, out, dres, dffn, ng_two = forward(
            turn * later, tokens, q, k, v, pre, init, cos, sin, table, w_out, w_up, w_down, norm_gains, norm_biases, cotangent
        )
        down_got = swap_core(unit_call(sc, hidden, dffn, False, block, True, False))
        down = unit_call(sc, hidden, dffn, True, block, True, False, down_got)
        dhid, dres_one, dbranch, dnum, dden, part, d_total, ng_one = backward(
            dffn, slope, dres, n0, rstd, mixed, inv, q, cos, sin, w_out, w_up, w_down, norm_gains
        )
        d_init = swap_core(d_total)
        up_got = swap_core(unit_call(sc, low, dhid, False, block, False, True))
        up = unit_call(sc, low, dhid, True, block, False, True, up_got)
        dq, dk, dv = attend_back(turn * (1.0 - later), q, k, v, dnum, dden, state, part, d_init, cos, sin, table, table_t)
        rest_a = jnp.concatenate([mixed, tokens, tokens, tokens], axis=1)
        rest_b = jnp.concatenate([dbranch, dq, dk, dv], axis=1)
        rest_got = swap_core(unit_call(sc, rest_a, rest_b, False, block, True, True))
        rest = unit_call(sc, rest_a, rest_b, True, block, True, True, rest_got)
        d_tokens = token_grad(dres_one, dq, dk, dv, w_query, w_key, w_value)

        down = reduce_units(down)
        up = reduce_units(up)
        rest = reduce_units(rest)
        down_other, up_other, rest_other = swap_core(down), swap_core(up), swap_core(rest)
        grad_down = gather_units(sc, down, down_other, block, True)
        grad_up = gather_units(sc, up, up_other, block, False)
        grads = [pick_unit(sc, rest, rest_other, u, block) for u in range(4)]

        norm = jnp.concatenate([ng_one, ng_two])
        norm = norm + swap_core(norm)
        norm = norm + swap_x(norm)
        norm = norm + swap_y(norm)
        if n_z & (n_z - 1) == 0:
            bit = 1
            while bit < n_z:
                norm = norm + swap_z(norm, bit)
                bit *= 2
        else:
            norm = lax.psum(norm, "dp", axis_index_groups=[[2 * i + j for i in range(n_z)] for j in range(2)])
        return (
            out, d_tokens, grads[1], grads[2], grads[3], grads[0], grad_up, grad_down,
            jnp.stack([norm[0], norm[2]]), jnp.stack([norm[1], norm[3]]),
        )

    return local


def solution(mesh):
    rows, whole = P(("dp", "head"), None), P()
    return jax.shard_map(
        make_local(mesh.shape["dp"], mesh.shape["head"]),
        mesh=mesh,
        in_specs=(rows,) + (whole,) * 8 + (rows,),
        out_specs=(rows, rows) + (whole,) * 8,
        check_vma=False,
    )
```

```python
import functools
import math

import jax
import jax.numpy as jnp
import numpy as np
from jax import lax
from jax.experimental import pallas as pl
from jax.experimental.pallas import tpu as pltpu
from jax.sharding import PartitionSpec as P

D = 768
E = 64
FF = 3072
LENGTH = 2048
CHUNK = 256
PAIR = 2 * E
PAIRS = D // PAIR
FEAT = 2 * PAIR
EPSILON = 1e-05
STEP_ANGLE = 0.5 * math.pi / LENGTH
HALF = D // 2
QUARTER = D // 4
LIMIT = 63 * 2**20
PACE = 1.0
WEIGHTS = dict(
    project=11, rows=60, attend_back=19, token_grad=10, gather_units=8, gather_qkv=5.5, gather_rest=4, add_cut=2.5, add_all=2, join=2
)

f32 = jnp.float32
bf16 = jnp.bfloat16


def nn(a, b):
    return jnp.dot(a, b, preferred_element_type=f32)


def tn(a, b):
    return lax.dot_general(a, b, (((0,), (0,)), ((), ())), preferred_element_type=f32)


def nt(a, b):
    return lax.dot_general(a, b, (((1,), (1,)), ((), ())), preferred_element_type=f32)


def ordered_call(
    kernel, name, grid, in_specs, out_specs, out_shape, scratch_shapes=(), scalars=0, deps=(),
):
    deps = list(deps)

    def body(*refs):
        first = scalars + len(in_specs)
        kernel(*refs[:first], *refs[first + len(deps) :])

    call = pl.pallas_call(
        body,
        grid_spec=pltpu.PrefetchScalarGridSpec(
            num_scalar_prefetch=scalars,
            grid=grid,
            in_specs=list(in_specs) + [pl.BlockSpec(memory_space=pl.ANY)] * len(deps),
            out_specs=out_specs,
            scratch_shapes=list(scratch_shapes),
        ),
        out_shape=out_shape,
        compiler_params=pltpu.CompilerParams(vmem_limit_bytes=LIMIT),
        cost_estimate=pl.CostEstimate(
            flops=int(PACE * WEIGHTS[name] * 1.15e9) + 1, bytes_accessed=1, transcendentals=0
        ),
        name=name,
    )
    return lambda *args: call(*args, *deps)


def whole(*shape):
    return pl.BlockSpec(shape, lambda *_: (0,) * len(shape))


def by_chunk(width, last=None):
    if last is None:
        return pl.BlockSpec((CHUNK, width), lambda i, *_: (i, 0))
    return pl.BlockSpec((CHUNK, width), lambda i, *_: (last - i, 0))


ANY = pl.BlockSpec(memory_space=pl.ANY)


def softplus(x):
    return jnp.maximum(x, 0.0) + jnp.log1p(jnp.exp(-jnp.abs(x)))


def lane_head(rows):
    return (lax.broadcasted_iota(jnp.int32, (rows, PAIR), 1) >= E).astype(jnp.int32)


def row_head():
    return (lax.broadcasted_iota(jnp.int32, (FEAT, PAIR), 0) % PAIR >= E).astype(jnp.int32)


def unpack_state(packed):
    same = row_head() == lane_head(FEAT)
    left = jnp.where(same, packed, 0.0)
    right = jnp.where(same, pltpu.roll(packed, E, 1), 0.0)
    return jnp.concatenate([left, right], axis=1).astype(bf16)


def features(x, cosine, sine):
    return jnp.concatenate([x * cosine, x * sine], axis=1).astype(bf16)


def with_ones(v):
    return jnp.concatenate([v, jnp.ones_like(v)], axis=1)


def turn_state(state, angle, on):
    cosine, sine = math.cos(angle) * on, math.sin(angle) * on
    first, second = state[:PAIR], state[PAIR:]
    return jnp.concatenate([cosine * first + sine * second, cosine * second - sine * first], axis=0)


def project_kernel(tok, wq, wk, wv, cos, sin, q_ref, k_ref, v_ref, pre_ref, tot_ref):
    @pl.when(pl.program_id(0) == 0)
    def _():
        tot_ref[...] = jnp.zeros_like(tot_ref)

    x = tok[...]
    q_ref[...] = softplus(nn(x, wq[...])).astype(bf16)
    k = softplus(nn(x, wk[...])).astype(bf16)
    k_ref[...] = k
    v = nn(x, wv[...]).astype(bf16)
    v_ref[...] = v
    same = row_head() == lane_head(FEAT)
    for p in range(PAIRS):
        cols = slice(p * PAIR, (p + 1) * PAIR)
        k_feat = features(k[:, cols].astype(f32), cos[...], sin[...])
        both = tn(k_feat, with_ones(v[:, cols]))
        pre_ref[0, p] = tot_ref[p]
        tot_ref[p] += jnp.where(same, both[:, :PAIR], both[:, PAIR:])


def project(tokens, wq, wk, wv, cos, sin):
    rows = tokens.shape[0]
    steps = rows // CHUNK
    act = jax.ShapeDtypeStruct((rows, D), bf16)
    return ordered_call(
        project_kernel,
        "project",
        grid=(steps,),
        in_specs=[by_chunk(D), whole(D, D), whole(D, D), whole(D, D), by_chunk(PAIR), by_chunk(PAIR)],
        out_specs=[
            by_chunk(D), by_chunk(D), by_chunk(D),
            pl.BlockSpec((1, PAIRS, FEAT, PAIR), lambda i: (i, 0, 0, 0)), whole(PAIRS, FEAT, PAIR),
        ],
        out_shape=[
            act, act, act,
            jax.ShapeDtypeStruct((steps, PAIRS, FEAT, PAIR), f32), jax.ShapeDtypeStruct((PAIRS, FEAT, PAIR), f32),
        ],
    )(tokens, wq, wk, wv, cos, sin)


def norm_parts(z):
    centred = z - jnp.mean(z, axis=-1, keepdims=True)
    rstd = lax.rsqrt(jnp.mean(centred * centred, axis=-1, keepdims=True) + EPSILON)
    return centred * rstd, rstd


def norm_back(t, n, rstd):
    return (t - jnp.mean(t, axis=-1, keepdims=True) - n * jnp.mean(t * n, axis=-1, keepdims=True)) * rstd


def rows_kernel(
    angle, block, sc, tok, q_ref, k_ref, v_ref, pre, init, cos, sin, table, w_out, w_up, w_down, gains, biases, cot,
    out_ref, dres_one_ref, dnum_ref, dden_ref, part_ref, tot_ref, one_own, one_other, two_own, two_first, two_second, two_rest,
    mixed, hid, slope, dhid, acc_down, acc_up, acc_out, ng, stage, norm_stage, sems, norm_sems,
):
    core = sc[0]
    step = pl.program_id(0)
    first = step == 0

    @pl.when(first)
    def _():
        ng[...] = jnp.zeros_like(ng)
        tot_ref[...] = jnp.zeros_like(tot_ref)

    later = core.astype(f32)
    second = lane_head(CHUNK) == 1
    second2 = jnp.concatenate([second, second], axis=1)
    inverse = []
    for p in range(PAIRS):
        cols = slice(p * PAIR, (p + 1) * PAIR)
        state = unpack_state(pre[0, p] + turn_state(init[p], angle, later))
        q, k, v = q_ref[:, cols], k_ref[:, cols], v_ref[:, cols]
        total = nn(features(q.astype(f32), cos[...], sin[...]), state)
        v_ones = with_ones(v)
        zero = jnp.zeros_like(q)
        score_0 = (nt(jnp.where(second, zero, q), k) * table[...]).astype(bf16)
        score_1 = (nt(jnp.where(second, q, zero), k) * table[...]).astype(bf16)
        total += jnp.where(second2, nn(score_1, v_ones), nn(score_0, v_ones))
        inv = 1.0 / total[:, PAIR:]
        inverse.append(inv)
        mixed[:, cols] = (total[:, :PAIR] * inv).astype(bf16)
    z = tok[...].astype(f32) + nn(mixed[...], w_out[...])
    n0, rstd0 = norm_parts(z)
    normed = n0 * gains[0:1] + biases[0:1]
    low = normed.astype(bf16)
    z = normed
    for j in range(FF // D):
        cols = slice(j * D, (j + 1) * D)
        h = nn(low, w_up[:, cols])
        phi = 0.5 * (1.0 + lax.erf(h * (0.5**0.5)))
        hid[:, cols] = (h * phi).astype(bf16)
        slope[:, cols] = phi + h * jnp.exp(-0.5 * h * h) * ((2 * math.pi) ** -0.5)
    z = normed + nn(hid[...], w_down[...])
    n1, rstd1 = norm_parts(z)
    out_ref[...] = (n1 * gains[1:2] + biases[1:2]).astype(bf16)
    g = cot[...].astype(f32)
    ng[2:3] += jnp.sum(g * n1, axis=0, keepdims=True)
    ng[3:4] += jnp.sum(g, axis=0, keepdims=True)
    dres = norm_back(g * gains[1:2], n1, rstd1)
    dffn = dres.astype(bf16)
    for j in range(FF // D):
        cols = slice(j * D, (j + 1) * D)
        dhid[:, cols] = (nt(dffn, w_down[cols, :]) * slope[:, cols]).astype(bf16)
    g = dres + nt(dhid[...], w_up[...])
    ng[0:1] += jnp.sum(g * n0, axis=0, keepdims=True)
    ng[1:2] += jnp.sum(g, axis=0, keepdims=True)
    dres_one = norm_back(g * gains[0:1], n0, rstd0)
    dres_one_ref[...] = dres_one
    dbranch = dres_one.astype(bf16)
    dmixed = nt(dbranch, w_out[...]).astype(bf16).astype(f32)
    lane = lax.broadcasted_iota(jnp.int32, (CHUNK, PAIR), 1)
    same = row_head() == lane_head(FEAT)
    for p in range(PAIRS):
        cols = slice(p * PAIR, (p + 1) * PAIR)
        dnum = (dmixed[:, cols] * inverse[p]).astype(bf16)
        dnum_ref[:, cols] = dnum
        moment = dnum.astype(f32) * mixed[:, cols].astype(f32)
        first_sum = jnp.sum(jnp.where(second, 0.0, moment), axis=1, keepdims=True)
        second_sum = jnp.sum(jnp.where(second, moment, 0.0), axis=1, keepdims=True)
        dden = jnp.where(second, second_sum, first_sum) * (-2.0 / E)
        high = dden.astype(bf16)
        rest = (dden - high.astype(f32)).astype(bf16)
        dden = jnp.where(lane % E < E // 2, high, rest)
        dden_ref[:, cols] = dden
        both = tn(features(q_ref[:, cols].astype(f32), cos[...], sin[...]), jnp.concatenate([dnum, dden], axis=1))
        part = jnp.where(same, both[:, :PAIR], pltpu.roll(both[:, PAIR:], E, 1))
        part_ref[0, p] = part
        tot_ref[p] += part
    for j in range(FF // D):
        cols = slice(j * D, (j + 1) * D)
        acc_down[cols, :] = jnp.where(first, 0.0, acc_down[cols, :]) + tn(hid[:, cols], dffn)
        acc_up[:, cols] = jnp.where(first, 0.0, acc_up[:, cols]) + tn(low, dhid[:, cols])
    acc_out[...] = jnp.where(first, 0.0, acc_out[...]) + tn(mixed[...], dbranch)

    @pl.when(step == pl.num_programs(0) - 1)
    def _():
        slots = stage.shape[0]
        jobs = []
        for j in range(4):
            jobs.append((acc_down.at[j * D : (j + 1) * D, :], j // 2, one_own, one_other, j % 2 * D, j % 2 * D, D))
        for j in range(4):
            jobs.append((acc_up.at[:, j * D : (j + 1) * D], j // 2, two_own, two_second if j % 2 else two_first, j % 2 * D, 0, D))
        for j in range(2):
            jobs.append((acc_out.at[:, j * HALF : (j + 1) * HALF], j, two_own, two_rest, 2 * D, 0, HALF))

        def move(i, do):
            _, owner, own, other, own_at, other_at, size = jobs[i]
            slot = i % slots

            def one(to, start):
                do(pltpu.make_async_copy(stage.at[slot, :, pl.ds(0, size)], to.at[:, pl.ds(start, size)], sems.at[slot]))

            @pl.when(core == owner)
            def _():
                one(own, own_at)

            @pl.when(core != owner)
            def _():
                one(other, other_at)

        for i, (acc, owner, _, _, _, _, size) in enumerate(jobs):
            if i >= slots:
                move(i - slots, lambda copy: copy.wait())
            me = jnp.where(core == owner, sc[1], sc[2])
            for b in range(D // block):
                to = pl.multiple_of((jnp.int32(b) ^ me) * block, block)
                stage[i % slots, pl.ds(to, block), :size] = acc[b * block : (b + 1) * block, :].astype(bf16)
            move(i, lambda copy: copy.start())
        norm_stage[...] = jnp.zeros_like(norm_stage)
        copies = []
        for i, (me, to, start) in enumerate(((sc[1], two_own, 2 * D + HALF), (sc[2], two_rest, HALF))):
            base = pl.multiple_of(me * block, block)
            rows = [ng[r : r + 1, j * PAIR : (j + 1) * PAIR] for r in range(4) for j in range(PAIRS)]
            rows.append(jnp.zeros((block - len(rows), PAIR), f32))
            norm_stage[i, pl.ds(base, block), :] = jnp.concatenate(rows, axis=0).astype(bf16)
            copy = pltpu.make_async_copy(norm_stage.at[i], to.at[:, pl.ds(start, PAIR)], norm_sems.at[i])
            copy.start()
            copies.append(copy)
        for i in range(len(jobs) - slots, len(jobs)):
            move(i, lambda copy: copy.wait())
        for copy in copies:
            copy.wait()


def rows_call(sc, tokens, q, k, v, pre, init, cos, sin, table, w_out, w_up, w_down, gains, biases, cot, block):
    rows = tokens.shape[0]
    steps = rows // CHUNK

    def make(width, dtype=bf16, height=rows):
        return jax.ShapeDtypeStruct((height, width), dtype)

    def once(*shape):
        return pl.BlockSpec(shape, lambda *_: (0,) * len(shape), pipeline_mode=pl.Buffered(1))

    chunk, thin = by_chunk(D), by_chunk(PAIR)
    states = pl.BlockSpec((1, PAIRS, FEAT, PAIR), lambda i, sc: (i, 0, 0, 0))
    one, two = 2 * D, 2 * D + HALF + PAIR
    return ordered_call(
        functools.partial(rows_kernel, STEP_ANGLE * rows, block),
        "rows",
        scalars=1,
        grid=(steps,),
        in_specs=[
            chunk, chunk, chunk, chunk, states, once(PAIRS, FEAT, PAIR), thin, thin, once(CHUNK, CHUNK),
            once(D, D), once(D, FF), once(FF, D), once(2, D), once(2, D), chunk,
        ],
        out_specs=[chunk, chunk, chunk, chunk, states, whole(PAIRS, FEAT, PAIR)] + [ANY] * 6,
        out_shape=[
            make(D), make(D, f32), make(D), make(D), jax.ShapeDtypeStruct((steps, PAIRS, FEAT, PAIR), f32),
            jax.ShapeDtypeStruct((PAIRS, FEAT, PAIR), f32),
            make(one, bf16, D), make(one, bf16, D), make(two, bf16, D), make(D, bf16, D), make(D, bf16, D),
            make(HALF + PAIR, bf16, D),
        ],
        scratch_shapes=[
            pltpu.VMEM((CHUNK, D), bf16), pltpu.VMEM((CHUNK, FF), bf16), pltpu.VMEM((CHUNK, FF), f32),
            pltpu.VMEM((CHUNK, FF), bf16), pltpu.VMEM((FF, D), f32), pltpu.VMEM((D, FF), f32), pltpu.VMEM((D, D), f32),
            pltpu.VMEM((4, D), f32), pltpu.VMEM((3, D, D), bf16), pltpu.VMEM((2, D, PAIR), bf16),
            pltpu.SemaphoreType.DMA((3,)), pltpu.SemaphoreType.DMA((2,)),
        ],
    )(sc, tokens, q, k, v, pre, init, cos, sin, table, w_out, w_up, w_down, gains, biases, cot)


def sigmoid_of(soft):
    return jnp.where(soft < 0.01, soft * (1.0 - 0.5 * soft), 1.0 - jnp.exp(-soft))


def attend_back_kernel(
    angle, block, own, sc, tok, q_ref, k_ref, v_ref, dnum_ref, dden_ref, pre, init, part, d_init, cos, sin, table, table_t,
    *refs,
):
    if own:
        *got, out_ref, keep_ref, send_ref, run, acc, wide = refs
    else:
        out_ref, *other_refs, run, acc = refs
    pairs = PAIRS // 2
    later = sc[0].astype(f32)

    @pl.when(pl.program_id(0) == 0)
    def _():
        for p in range(pairs):
            run[p] = turn_state(d_init[p], -angle, 1.0 - later)

    second = lane_head(CHUNK) == 1
    second2 = jnp.concatenate([second, second], axis=1)

    def split(x, mask):
        zero = jnp.zeros_like(x)
        return jnp.where(mask, zero, x), jnp.where(mask, x, zero)

    for p in range(pairs):
        cols = slice(p * PAIR, (p + 1) * PAIR)
        q, k, v = q_ref[:, cols], k_ref[:, cols], v_ref[:, cols]
        q_wide, k_wide = q.astype(f32), k.astype(f32)
        dnum = dnum_ref[:, cols]
        grad = jnp.concatenate([dnum, dden_ref[:, cols]], axis=1)
        v_ones = with_ones(v)
        state = unpack_state(pre[0, p] + turn_state(init[p], angle, later))
        d_state = unpack_state(run[p])
        run[p] += part[0, p]
        dq_feat = nt(grad, state)
        dk_feat = nt(v_ones, d_state)
        dv = nn(features(k_wide, cos[...], sin[...]), d_state[:, :PAIR])
        dq = dq_feat[:, :PAIR] * cos[...] + dq_feat[:, PAIR:] * sin[...]
        dk = dk_feat[:, :PAIR] * cos[...] + dk_feat[:, PAIR:] * sin[...]
        for grad_h, q_h, k_h, dnum_h in zip(split(grad, second2), split(q, second), split(k, second), split(dnum, second)):
            d_score = (nt(grad_h, v_ones) * table[...]).astype(bf16)
            dq += nn(d_score, k_h)
            score_t = (nt(k_h, q) * table_t[...]).astype(bf16)
            d_score_t = (nt(v_ones, grad_h) * table_t[...]).astype(bf16)
            dk += nn(d_score_t, q_h)
            dv += nn(score_t, dnum_h)
        out_ref[:, cols] = (dq.astype(bf16).astype(f32) * sigmoid_of(q_wide)).astype(bf16)
        out_ref[:, slice(HALF + p * PAIR, HALF + (p + 1) * PAIR)] = (
            dk.astype(bf16).astype(f32) * sigmoid_of(k_wide)
        ).astype(bf16)
        out_ref[:, slice(D + p * PAIR, D + (p + 1) * PAIR)] = dv.astype(bf16)
    acc[...] = jnp.where(pl.program_id(0) == 0, 0.0, acc[...]) + tn(tok[...], out_ref[...])

    @pl.when(pl.program_id(0) == pl.num_programs(0) - 1)
    def _():
        me = sc[1] if own else sc[2]
        for b in range(D // block):
            to = pl.ds(pl.multiple_of((jnp.int32(b) ^ me) * block, block), block)
            for j in range(3):
                cols = slice(j * HALF, (j + 1) * HALF)
                piece = acc[b * block : (b + 1) * block, cols]
                if own:
                    wide[to, cols] = (piece + got[j][to, :].astype(f32)).astype(bf16)
                else:
                    other_refs[j][to, :] = piece.astype(bf16)
        if own:
            keep_ref[...] = wide[:HALF]
            send_ref[...] = wide[HALF:]


def attend_back(
    sc, tokens, q, k, v, dnum, dden, pre, init, part, d_init, cos, sin, table, table_t, block, got=None, deps=()
):
    own = got is not None
    rows = q.shape[0]
    steps = rows // CHUNK
    last = steps - 1
    pairs = PAIRS // 2

    def half(sc):
        return sc[0] if own else 1 - sc[0]

    def make(height):
        return jax.ShapeDtypeStruct((height, 3 * HALF), bf16)

    chunk = pl.BlockSpec((CHUNK, HALF), lambda i, sc: (last - i, half(sc)))
    states = pl.BlockSpec((1, pairs, FEAT, PAIR), lambda i, sc: (last - i, half(sc), 0, 0))
    state = pl.BlockSpec((pairs, FEAT, PAIR), lambda i, sc: (half(sc), 0, 0))
    thin = by_chunk(PAIR, last)
    return ordered_call(
        functools.partial(attend_back_kernel, STEP_ANGLE * rows, block, own),
        "attend_back",
        scalars=1,
        deps=deps,
        grid=(steps,),
        in_specs=[
            by_chunk(D, last), chunk, chunk, chunk, chunk, chunk, states, state, states, state, thin, thin,
            whole(CHUNK, CHUNK), whole(CHUNK, CHUNK),
        ] + [whole(D, HALF)] * (3 * own),
        out_specs=[by_chunk(3 * HALF, last)] + ([whole(HALF, 3 * HALF)] * 2 if own else [whole(D, HALF)] * 3),
        out_shape=[make(rows)] + ([make(HALF)] * 2 if own else [jax.ShapeDtypeStruct((D, HALF), bf16)] * 3),
        scratch_shapes=[pltpu.VMEM((pairs, FEAT, PAIR), f32), pltpu.VMEM((D, 3 * HALF), f32)]
        + [pltpu.VMEM((D, 3 * HALF), bf16)] * own,
    )(sc, tokens, q, k, v, dnum, dden, pre, init, part, d_init, cos, sin, table, table_t, *(got or ()))


def token_grad_kernel(sc, dres_one, first, second, wq1, wk1, wv1, wq2, wk2, wv2, out):
    total = dres_one[...]
    for d, weights in ((first, (wq1, wk1, wv1)), (second, (wq2, wk2, wv2))):
        for j, w in enumerate(weights):
            total += nt(d[:, j * HALF : (j + 1) * HALF], w[...])
    out[...] = total


def token_grad(sc, dres_one, other, own, wq, wk, wv, deps=()):
    rows = own.shape[0]
    w_other = pl.BlockSpec((D, HALF), lambda i, sc: (0, 1 - sc[0]))
    w_own = pl.BlockSpec((D, HALF), lambda i, sc: (0, sc[0]))
    return ordered_call(
        token_grad_kernel,
        "token_grad",
        scalars=1,
        deps=deps,
        grid=(rows // CHUNK,),
        in_specs=[by_chunk(D), by_chunk(3 * HALF), by_chunk(3 * HALF)] + [w_other] * 3 + [w_own] * 3,
        out_specs=by_chunk(D),
        out_shape=jax.ShapeDtypeStruct((rows, D), f32),
    )(sc, dres_one, other, own, wq, wk, wv, wq, wk, wv)


def small_call(kernel, ins, out_rows, name, deps=()):
    width = ins[0].shape[1]
    many = isinstance(out_rows, (list, tuple))

    def shape(rows):
        return jax.ShapeDtypeStruct((rows, width), bf16)

    return ordered_call(
        kernel,
        name,
        deps=deps,
        grid=(1,),
        in_specs=[whole(*x.shape) for x in ins],
        out_specs=[whole(r, width) for r in out_rows] if many else whole(out_rows, width),
        out_shape=[shape(r) for r in out_rows] if many else shape(out_rows),
    )(*ins)


def add_cut_kernel(a, b, *outs):
    rows = outs[0].shape[0]
    for i, out in enumerate(outs):
        at = slice(i * rows, (i + 1) * rows)
        out[...] = (a[at].astype(f32) + b[at].astype(f32)).astype(bf16)


def add_cut_parts_kernel(a, first, second, rest, keep, send):
    start = 0
    for part in (first, second, rest):
        cols = slice(start, start + part.shape[1])
        keep[:, cols] = (a[:HALF, cols].astype(f32) + part[:HALF].astype(f32)).astype(bf16)
        send[:, cols] = (a[HALF:, cols].astype(f32) + part[HALF:].astype(f32)).astype(bf16)
        start += part.shape[1]


def add_all_kernel(*refs):
    total = refs[0][...].astype(f32)
    for ref in refs[1:-1]:
        total += ref[...].astype(f32)
    refs[-1][...] = total.astype(bf16)


def join_kernel(*refs):
    rows = refs[0].shape[0]
    for i, ref in enumerate(refs[:-1]):
        refs[-1][i * rows : (i + 1) * rows] = ref[...]


def add_cut(a, b, parts, deps=()):
    return small_call(add_cut_kernel, [a, b], [a.shape[0] // parts] * parts, "add_cut", deps)


def add_all(parts, deps=()):
    return small_call(add_all_kernel, parts, parts[0].shape[0], "add_all", deps)


def join(parts, deps=()):
    return small_call(join_kernel, parts, len(parts) * parts[0].shape[0], "join", deps)


def restore(me, block, quarters, put):
    for place in range(D // block):
        ref, at = quarters[place * block // QUARTER], place * block % QUARTER
        put(pl.multiple_of((jnp.int32(place) ^ me) * block, block), ref[at : at + block, :].astype(f32))


def gather_kernel(block, per_core, sc, *refs):
    mine, other, out = refs[:4], refs[4:8], refs[8]

    def put(row, piece):
        out[pl.ds(row, block), :] = piece

    is_mine = pl.program_id(0) // per_core == sc[0]

    @pl.when(is_mine)
    def _():
        restore(sc[1], block, mine, put)

    @pl.when(jnp.logical_not(is_mine))
    def _():
        restore(sc[2], block, other, put)


def gather_units(sc, parts, block, by_rows, deps=()):
    def at(own):
        def index(g, sc):
            return (0, jnp.clip(g - 2 * (sc[0] if own else 1 - sc[0]), 0, 1))

        return pl.BlockSpec((QUARTER, D), index)

    return ordered_call(
        functools.partial(gather_kernel, block, 2),
        "gather_units",
        scalars=1,
        deps=deps,
        grid=(4,),
        in_specs=[at(True)] * 4 + [at(False)] * 4,
        out_specs=pl.BlockSpec((D, D), (lambda g, sc: (g, 0)) if by_rows else (lambda g, sc: (0, g))),
        out_shape=jax.ShapeDtypeStruct((4 * D, D) if by_rows else (D, 4 * D), f32),
    )(sc, *parts)


def half_of(block, sc, group, start, size, store):
    mine, other = group[:4], group[4:]

    def cut(refs):
        return [ref.at[:, start : start + size] for ref in refs]

    is_mine = pl.program_id(0) == sc[0]

    @pl.when(is_mine)
    def _():
        restore(sc[1], block, cut(mine), store)

    @pl.when(jnp.logical_not(is_mine))
    def _():
        restore(sc[2], block, cut(other), store)


def gather_qkv_kernel(block, sc, *refs):
    for j, out in enumerate(refs[8:]):
        def put(row, piece, out=out):
            out[pl.ds(row, block), :] = piece

        half_of(block, sc, refs[:8], j * HALF, HALF, put)


def gather_qkv(sc, parts, block, deps=()):
    shape = jax.ShapeDtypeStruct((D, D), f32)
    return ordered_call(
        functools.partial(gather_qkv_kernel, block),
        "gather_qkv",
        scalars=1,
        deps=deps,
        grid=(2,),
        in_specs=[whole(QUARTER, 3 * HALF)] * 8,
        out_specs=[pl.BlockSpec((D, HALF), lambda g, sc: (0, g))] * 3,
        out_shape=[shape] * 3,
    )(sc, *parts)


def gather_rest_kernel(block, sc, *refs):
    group, out, gains, biases, rows = refs[:8], *refs[8:]

    def put(row, piece):
        out[pl.ds(row, block), :] = piece

    def put_norm(row, piece):
        rows[pl.ds(row, block), :] = piece

    half_of(block, sc, group, 0, HALF, put)

    @pl.when(pl.program_id(0) == 0)
    def _():
        half_of(block, sc, group, HALF, PAIR, put_norm)
        for i in range(2):
            for j in range(PAIRS):
                cols = slice(j * PAIR, (j + 1) * PAIR)
                first, second = 2 * i * PAIRS + j, (2 * i + 1) * PAIRS + j
                gains[i : i + 1, cols] = rows[first : first + 1, :]
                biases[i : i + 1, cols] = rows[second : second + 1, :]


def gather_rest(sc, parts, block, deps=()):
    norm = jax.ShapeDtypeStruct((2, D), f32)
    spec = pl.BlockSpec((QUARTER, HALF + PAIR), lambda g, sc: (0, 2 * D // (HALF + PAIR)))
    return ordered_call(
        functools.partial(gather_rest_kernel, block),
        "gather_rest",
        scalars=1,
        deps=deps,
        grid=(2,),
        in_specs=[spec] * 8,
        out_specs=[pl.BlockSpec((D, HALF), lambda g, sc: (0, g)), whole(2, D), whole(2, D)],
        out_shape=[jax.ShapeDtypeStruct((D, D), f32), norm, norm],
        scratch_shapes=[pltpu.VMEM((D, PAIR), f32)],
    )(sc, *parts)


def make_local(n_dp, n_head):
    n_z = n_dp // 2
    direct = QUARTER % (16 * n_z) == 0 and n_z & (n_z - 1) == 0
    places = n_z if direct else 1
    block = QUARTER // places
    both_axes = ("dp", "head")

    def swap(x, partner):
        pairs = []
        for d in range(n_dp):
            for h in range(n_head):
                to_d, to_h = partner(d, h)
                pairs.append((d * n_head + h, to_d * n_head + to_h))
        return lax.ppermute(x, both_axes, pairs)

    def swap_core(x):
        return swap(x, lambda d, h: (d, h ^ 1))

    def swap_first(x):
        return swap(x, lambda d, h: (d ^ 1, h) if h % 2 else (d, h ^ 2))

    def swap_second(x):
        return swap(x, lambda d, h: (d, h ^ 2) if h % 2 else (d ^ 1, h))

    def swap_z(x, k):
        return swap(x, lambda d, h: (d ^ (2 * k), h))

    def cut_z(keep, got, deps=()):
        if direct:
            parts = add_cut(keep, got, n_z, deps)
            return [parts[0]] + [swap_z(parts[i], i) for i in range(1, n_z)]
        both = keep.astype(f32) + got.astype(f32)
        same_z = [[2 * i + j for i in range(n_z)] for j in range(2)]
        return lax.psum(both, "dp", axis_index_groups=same_z).astype(bf16)

    def share_z(parts, deps=()):
        if not direct:
            return parts
        share = add_all(parts, deps)
        return [share] + [swap_z(share, i) for i in range(1, n_z)]

    def spread(parts, deps=()):
        own = join(parts, deps) if direct else parts
        second = swap_second(own)
        first = swap_first(own)
        both = swap_first(second)
        quarters = [own, second, first, both]
        return quarters + [swap_core(x) for x in quarters]

    def local(tokens, w_query, w_key, w_value, w_out, w_up, w_down, norm_gains, norm_biases, cotangent):
        rows = tokens.shape[0]
        assert LENGTH == 2 * rows and n_head % 4 == 0 and n_dp % 2 == 0
        head, dp = lax.axis_index("head"), lax.axis_index("dp")
        core, x, y, z = head % 2, head // 2, dp % 2, dp // 2
        rank = z if direct else 0
        by_x, by_y = (2 * x + y) * places + rank, (2 * y + x) * places + rank
        sc = jnp.stack([core, jnp.where(core == 0, by_x, by_y), jnp.where(core == 0, by_y, by_x)]).astype(jnp.int32)
        angle = STEP_ANGLE * np.arange(rows)
        cos = jnp.asarray(np.broadcast_to(np.cos(angle)[:, None], (rows, PAIR)), f32)
        sin = jnp.asarray(np.broadcast_to(np.sin(angle)[:, None], (rows, PAIR)), f32)
        gap = np.arange(CHUNK)[:, None] - np.arange(CHUNK)[None, :]
        weights = np.where(gap >= 0, np.cos(STEP_ANGLE * gap), 0.0)
        table, table_t = jnp.asarray(weights, f32), jnp.asarray(weights.T, f32)

        q, k, v, pre, total = project(tokens, w_query, w_key, w_value, cos, sin)
        init = swap_core(total)
        out, dres_one, dnum, dden, part, d_total, one_own, one_other, two_own, *two_other = rows_call(
            sc, tokens, q, k, v, pre, init, cos, sin, table, w_out, w_up, w_down, norm_gains, norm_biases, cotangent, block
        )
        one_got = swap_core(one_other)
        d_init = swap_core(d_total)
        two_got = [swap_core(x) for x in two_other]
        one_keep, one_send = add_cut(one_own, one_got, 2)
        one_got = swap_first(one_send)
        two_keep, two_send = small_call(
            add_cut_parts_kernel, [two_own, *two_got], [HALF, HALF], "add_cut", deps=(one_keep,)
        )
        two_got = swap_first(two_send)
        att = functools.partial(
            attend_back, sc, tokens, q, k, v, dnum, dden, pre, init, part, d_init, cos, sin, table, table_t, block
        )
        d_other, *three_other = att(deps=(two_keep,))
        three_got = [swap_core(x) for x in three_other]
        one_keep, one_send = add_cut(one_keep, one_got, 2, deps=(d_other,))
        one_got = swap_second(one_send)
        two_keep, two_send = add_cut(two_keep, two_got, 2, deps=(one_keep,))
        two_got = swap_second(two_send)
        d_own, three_keep, three_send = att(three_got, deps=(two_keep,))
        three_got = swap_first(three_send)
        one_parts = cut_z(one_keep, one_got, deps=(three_keep,))
        two_parts = cut_z(two_keep, two_got, deps=(one_parts[0],))
        d_tokens = token_grad(sc, dres_one, d_other, d_own, w_query, w_key, w_value, deps=(two_parts[0],))
        three_keep, three_send = add_cut(three_keep, three_got, 2, deps=(d_tokens,))
        three_got = swap_second(three_send)
        one_parts = share_z(one_parts, deps=(three_keep,))
        three_parts = cut_z(three_keep, three_got, deps=(one_parts[0],))
        two_parts = share_z(two_parts, deps=(three_parts[0],))
        one_parts = spread(one_parts, deps=(two_parts[0],))
        three_parts = share_z(three_parts, deps=(one_parts[0],))
        two_parts = spread(two_parts, deps=(three_parts[0],))
        three_parts = spread(three_parts, deps=(two_parts[0],))
        grad_down = gather_units(sc, one_parts, block, True, deps=(three_parts[0],))
        grad_up = gather_units(sc, two_parts, block, False, deps=(grad_down,))
        grad_out, grad_gains, grad_biases = gather_rest(sc, two_parts, block, deps=(grad_up,))
        grad_qkv = gather_qkv(sc, three_parts, block, deps=(grad_out,))
        return out, d_tokens, *grad_qkv, grad_out, grad_up, grad_down, grad_gains, grad_biases

    return local


def solution(mesh):
    rows, same = P(("dp", "head"), None), P()
    return jax.shard_map(
        make_local(mesh.shape["dp"], mesh.shape["head"]),
        mesh=mesh,
        in_specs=(rows,) + (same,) * 8 + (rows,),
        out_specs=(rows, rows) + (same,) * 8,
        check_vma=False,
    )
```

```python
import functools
import math

import jax
import jax.numpy as jnp
import numpy as np
from jax import lax
from jax.experimental import pallas as pl
from jax.experimental.pallas import tpu as pltpu
from jax.sharding import PartitionSpec as P

D = 768
E = 64
FF = 3072
LENGTH = 2048
CHUNK = 256
PAIR = 2 * E
PAIRS = D // PAIR
FEAT = 2 * PAIR
EPSILON = 1e-05
STEP_ANGLE = 0.5 * math.pi / LENGTH
HALF = D // 2
QUARTER = D // 4
LIMIT = 63 * 2**20
PACE = 1.0
WEIGHTS = dict(
    project=11, rows=60, attend_back=19, token_grad=10, gather_units=8, gather_qkv=5.5, gather_rest=4, add_cut=2.5, add_all=2, join=2
)

f32 = jnp.float32
bf16 = jnp.bfloat16


def nn(a, b):
    return jnp.dot(a, b, preferred_element_type=f32)


def tn(a, b):
    return lax.dot_general(a, b, (((0,), (0,)), ((), ())), preferred_element_type=f32)


def nt(a, b):
    return lax.dot_general(a, b, (((1,), (1,)), ((), ())), preferred_element_type=f32)


def ordered_call(
    kernel, name, grid, in_specs, out_specs, out_shape, scratch_shapes=(), scalars=0, deps=(),
):
    deps = list(deps)

    def body(*refs):
        first = scalars + len(in_specs)
        kernel(*refs[:first], *refs[first + len(deps) :])

    call = pl.pallas_call(
        body,
        grid_spec=pltpu.PrefetchScalarGridSpec(
            num_scalar_prefetch=scalars,
            grid=grid,
            in_specs=list(in_specs) + [pl.BlockSpec(memory_space=pl.ANY)] * len(deps),
            out_specs=out_specs,
            scratch_shapes=list(scratch_shapes),
        ),
        out_shape=out_shape,
        compiler_params=pltpu.CompilerParams(vmem_limit_bytes=LIMIT),
        cost_estimate=pl.CostEstimate(
            flops=int(PACE * WEIGHTS[name] * 1.15e9) + 1, bytes_accessed=1, transcendentals=0
        ),
        name=name,
    )
    return lambda *args: call(*args, *deps)


def whole(*shape):
    return pl.BlockSpec(shape, lambda *_: (0,) * len(shape))


def by_chunk(width, last=None):
    if last is None:
        return pl.BlockSpec((CHUNK, width), lambda i, *_: (i, 0))
    return pl.BlockSpec((CHUNK, width), lambda i, *_: (last - i, 0))


ANY = pl.BlockSpec(memory_space=pl.ANY)


def softplus(x):
    return jnp.maximum(x, 0.0) + jnp.log1p(jnp.exp(-jnp.abs(x)))


def lane_head(rows):
    return (lax.broadcasted_iota(jnp.int32, (rows, PAIR), 1) >= E).astype(jnp.int32)


def row_head():
    return (lax.broadcasted_iota(jnp.int32, (FEAT, PAIR), 0) % PAIR >= E).astype(jnp.int32)


def unpack_state(packed):
    same = row_head() == lane_head(FEAT)
    left = jnp.where(same, packed, 0.0)
    right = jnp.where(same, pltpu.roll(packed, E, 1), 0.0)
    return jnp.concatenate([left, right], axis=1).astype(bf16)


def features(x, cosine, sine):
    return jnp.concatenate([x * cosine, x * sine], axis=1).astype(bf16)


def with_ones(v):
    return jnp.concatenate([v, jnp.ones_like(v)], axis=1)


def heads_apart(x, second):
    zero = jnp.zeros_like(x)
    return jnp.concatenate([jnp.where(second, zero, x), jnp.where(second, x, zero)], axis=0)


def turn_state(state, angle, on):
    cosine, sine = math.cos(angle) * on, math.sin(angle) * on
    first, second = state[:PAIR], state[PAIR:]
    return jnp.concatenate([cosine * first + sine * second, cosine * second - sine * first], axis=0)


def project_kernel(tok, wq, wk, wv, cos, sin, q_ref, k_ref, v_ref, pre_ref, tot_ref):
    @pl.when(pl.program_id(0) == 0)
    def _():
        tot_ref[...] = jnp.zeros_like(tot_ref)

    x = tok[...]
    q_ref[...] = softplus(nn(x, wq[...])).astype(bf16)
    k = softplus(nn(x, wk[...])).astype(bf16)
    k_ref[...] = k
    v = nn(x, wv[...]).astype(bf16)
    v_ref[...] = v
    same = row_head() == lane_head(FEAT)
    for p in range(PAIRS):
        cols = slice(p * PAIR, (p + 1) * PAIR)
        k_feat = features(k[:, cols].astype(f32), cos[...], sin[...])
        both = tn(k_feat, with_ones(v[:, cols]))
        pre_ref[0, p] = tot_ref[p]
        tot_ref[p] += jnp.where(same, both[:, :PAIR], both[:, PAIR:])


def project(tokens, wq, wk, wv, cos, sin):
    rows = tokens.shape[0]
    steps = rows // CHUNK
    act = jax.ShapeDtypeStruct((rows, D), bf16)
    return ordered_call(
        project_kernel,
        "project",
        grid=(steps,),
        in_specs=[by_chunk(D), whole(D, D), whole(D, D), whole(D, D), by_chunk(PAIR), by_chunk(PAIR)],
        out_specs=[
            by_chunk(D), by_chunk(D), by_chunk(D),
            pl.BlockSpec((1, PAIRS, FEAT, PAIR), lambda i: (i, 0, 0, 0)), whole(PAIRS, FEAT, PAIR),
        ],
        out_shape=[
            act, act, act,
            jax.ShapeDtypeStruct((steps, PAIRS, FEAT, PAIR), f32), jax.ShapeDtypeStruct((PAIRS, FEAT, PAIR), f32),
        ],
    )(tokens, wq, wk, wv, cos, sin)


def norm_parts(z):
    centred = z - jnp.mean(z, axis=-1, keepdims=True)
    rstd = lax.rsqrt(jnp.mean(centred * centred, axis=-1, keepdims=True) + EPSILON)
    return centred * rstd, rstd


def norm_back(t, n, rstd):
    return (t - jnp.mean(t, axis=-1, keepdims=True) - n * jnp.mean(t * n, axis=-1, keepdims=True)) * rstd


def rows_kernel(
    angle, block, sc, tok, q_ref, k_ref, v_ref, pre, init, cos, sin, table, w_out, w_up_hbm, w_down_hbm, gains, biases, cot,
    out_ref, dres_one_ref, dnum_ref, dden_ref, part_ref, tot_ref, one_own, one_other, two_own, two_first, two_second, two_rest,
    w_up, w_down, mixed, hid, slope, dhid, acc_down, acc_up, acc_out, ng, stage, norm_stage, sems, norm_sems, w_sems,
):
    core = sc[0]
    step = pl.program_id(0)
    first = step == 0

    def weight_copies():
        return (
            pltpu.make_async_copy(w_up_hbm, w_up, w_sems.at[0]),
            pltpu.make_async_copy(w_down_hbm, w_down, w_sems.at[1]),
        )

    @pl.when(first)
    def _():
        for copy in weight_copies():
            copy.start()
        ng[...] = jnp.zeros_like(ng)
        tot_ref[...] = jnp.zeros_like(tot_ref)

    later = core.astype(f32)
    second = lane_head(CHUNK) == 1
    second2 = jnp.concatenate([second, second], axis=1)
    inverse = []
    for p in range(PAIRS):
        cols = slice(p * PAIR, (p + 1) * PAIR)
        state = unpack_state(pre[0, p] + turn_state(init[p], angle, later))
        q, k, v = q_ref[:, cols], k_ref[:, cols], v_ref[:, cols]
        total = nn(features(q.astype(f32), cos[...], sin[...]), state)
        scores = (nt(q, heads_apart(k, second)) * table[...]).astype(bf16)
        total += nn(scores, heads_apart(with_ones(v), second2))
        inv = 1.0 / total[:, PAIR:]
        inverse.append(inv)
        mixed[:, cols] = (total[:, :PAIR] * inv).astype(bf16)
    z = tok[...].astype(f32) + nn(mixed[...], w_out[...])
    n0, rstd0 = norm_parts(z)
    normed = n0 * gains[0:1] + biases[0:1]
    low = normed.astype(bf16)

    @pl.when(first)
    def _():
        for copy in weight_copies():
            copy.wait()

    for j in range(FF // D):
        cols = slice(j * D, (j + 1) * D)
        h = nn(low, w_up[:, cols])
        phi = 0.5 * (1.0 + lax.erf(h * (0.5**0.5)))
        hid[:, cols] = (h * phi).astype(bf16)
        slope[:, cols] = phi + h * jnp.exp(-0.5 * h * h) * ((2 * math.pi) ** -0.5)
    z = normed + nn(hid[...], w_down[...])
    n1, rstd1 = norm_parts(z)
    out_ref[...] = (n1 * gains[1:2] + biases[1:2]).astype(bf16)
    g = cot[...].astype(f32)
    ng[2:3] += jnp.sum(g * n1, axis=0, keepdims=True)
    ng[3:4] += jnp.sum(g, axis=0, keepdims=True)
    dres = norm_back(g * gains[1:2], n1, rstd1)
    dffn = dres.astype(bf16)
    for j in range(FF // D):
        cols = slice(j * D, (j + 1) * D)
        dhid[:, cols] = (nt(dffn, w_down[cols, :]) * slope[:, cols]).astype(bf16)
    g = dres + nt(dhid[...], w_up[...])
    ng[0:1] += jnp.sum(g * n0, axis=0, keepdims=True)
    ng[1:2] += jnp.sum(g, axis=0, keepdims=True)
    dres_one = norm_back(g * gains[0:1], n0, rstd0)
    dres_one_ref[...] = dres_one
    dbranch = dres_one.astype(bf16)
    dmixed = nt(dbranch, w_out[...]).astype(bf16).astype(f32)
    lane = lax.broadcasted_iota(jnp.int32, (CHUNK, PAIR), 1)
    same = row_head() == lane_head(FEAT)
    for p in range(PAIRS):
        cols = slice(p * PAIR, (p + 1) * PAIR)
        dnum = (dmixed[:, cols] * inverse[p]).astype(bf16)
        dnum_ref[:, cols] = dnum
        moment = dnum.astype(f32) * mixed[:, cols].astype(f32)
        first_sum = jnp.sum(jnp.where(second, 0.0, moment), axis=1, keepdims=True)
        second_sum = jnp.sum(jnp.where(second, moment, 0.0), axis=1, keepdims=True)
        dden = jnp.where(second, second_sum, first_sum) * (-2.0 / E)
        high = dden.astype(bf16)
        rest = (dden - high.astype(f32)).astype(bf16)
        dden = jnp.where(lane % E < E // 2, high, rest)
        dden_ref[:, cols] = dden
        both = tn(features(q_ref[:, cols].astype(f32), cos[...], sin[...]), jnp.concatenate([dnum, dden], axis=1))
        part = jnp.where(same, both[:, :PAIR], pltpu.roll(both[:, PAIR:], E, 1))
        part_ref[0, p] = part
        tot_ref[p] += part
    for j in range(FF // D):
        cols = slice(j * D, (j + 1) * D)
        acc_down[cols, :] = jnp.where(first, 0.0, acc_down[cols, :]) + tn(hid[:, cols], dffn)
        acc_up[:, cols] = jnp.where(first, 0.0, acc_up[:, cols]) + tn(low, dhid[:, cols])
    acc_out[...] = jnp.where(first, 0.0, acc_out[...]) + tn(mixed[...], dbranch)

    @pl.when(step == pl.num_programs(0) - 1)
    def _():
        slots = stage.shape[0]
        jobs = []
        for j in range(4):
            jobs.append((acc_down.at[j * D : (j + 1) * D, :], j // 2, one_own, one_other, j % 2 * D, j % 2 * D, D))
        for j in range(4):
            jobs.append((acc_up.at[:, j * D : (j + 1) * D], j // 2, two_own, two_second if j % 2 else two_first, j % 2 * D, 0, D))
        for j in range(2):
            jobs.append((acc_out.at[:, j * HALF : (j + 1) * HALF], j, two_own, two_rest, 2 * D, 0, HALF))

        def move(i, do):
            _, owner, own, other, own_at, other_at, size = jobs[i]
            slot = i % slots

            def one(to, start):
                do(pltpu.make_async_copy(stage.at[slot, :, pl.ds(0, size)], to.at[:, pl.ds(start, size)], sems.at[slot]))

            @pl.when(core == owner)
            def _():
                one(own, own_at)

            @pl.when(core != owner)
            def _():
                one(other, other_at)

        for i, (acc, owner, _, _, _, _, size) in enumerate(jobs):
            if i >= slots:
                move(i - slots, lambda copy: copy.wait())
            me = jnp.where(core == owner, sc[3 if i < 4 else 1], sc[4 if i < 4 else 2])
            for b in range(D // block):
                to = pl.multiple_of((jnp.int32(b) ^ me) * block, block)
                stage[i % slots, pl.ds(to, block), :size] = acc[b * block : (b + 1) * block, :].astype(bf16)
            move(i, lambda copy: copy.start())
        norm_stage[...] = jnp.zeros_like(norm_stage)
        copies = []
        for i, (me, to, start) in enumerate(((sc[1], two_own, 2 * D + HALF), (sc[2], two_rest, HALF))):
            base = pl.multiple_of(me * block, block)
            rows = [ng[r : r + 1, j * PAIR : (j + 1) * PAIR] for r in range(4) for j in range(PAIRS)]
            rows.append(jnp.zeros((block - len(rows), PAIR), f32))
            norm_stage[i, pl.ds(base, block), :] = jnp.concatenate(rows, axis=0).astype(bf16)
            copy = pltpu.make_async_copy(norm_stage.at[i], to.at[:, pl.ds(start, PAIR)], norm_sems.at[i])
            copy.start()
            copies.append(copy)
        for i in range(len(jobs) - slots, len(jobs)):
            move(i, lambda copy: copy.wait())
        for copy in copies:
            copy.wait()


def rows_call(sc, tokens, q, k, v, pre, init, cos, sin, table, w_out, w_up, w_down, gains, biases, cot, block):
    rows = tokens.shape[0]
    steps = rows // CHUNK

    def make(width, dtype=bf16, height=rows):
        return jax.ShapeDtypeStruct((height, width), dtype)

    def once(*shape):
        return pl.BlockSpec(shape, lambda *_: (0,) * len(shape), pipeline_mode=pl.Buffered(1))

    chunk, thin = by_chunk(D), by_chunk(PAIR)
    states = pl.BlockSpec((1, PAIRS, FEAT, PAIR), lambda i, sc: (i, 0, 0, 0))
    one, two = 2 * D, 2 * D + HALF + PAIR
    return ordered_call(
        functools.partial(rows_kernel, STEP_ANGLE * rows, block),
        "rows",
        scalars=1,
        grid=(steps,),
        in_specs=[
            chunk, chunk, chunk, chunk, states, once(PAIRS, FEAT, PAIR), thin, thin, once(CHUNK, 2 * CHUNK),
            once(D, D), ANY, ANY, once(2, D), once(2, D), chunk,
        ],
        out_specs=[chunk, chunk, chunk, chunk, states, whole(PAIRS, FEAT, PAIR)] + [ANY] * 6,
        out_shape=[
            make(D), make(D, f32), make(D), make(D), jax.ShapeDtypeStruct((steps, PAIRS, FEAT, PAIR), f32),
            jax.ShapeDtypeStruct((PAIRS, FEAT, PAIR), f32),
            make(one, bf16, D), make(one, bf16, D), make(two, bf16, D), make(D, bf16, D), make(D, bf16, D),
            make(HALF + PAIR, bf16, D),
        ],
        scratch_shapes=[
            pltpu.VMEM((D, FF), bf16), pltpu.VMEM((FF, D), bf16),
            pltpu.VMEM((CHUNK, D), bf16), pltpu.VMEM((CHUNK, FF), bf16), pltpu.VMEM((CHUNK, FF), f32),
            pltpu.VMEM((CHUNK, FF), bf16), pltpu.VMEM((FF, D), f32), pltpu.VMEM((D, FF), f32), pltpu.VMEM((D, D), f32),
            pltpu.VMEM((4, D), f32), pltpu.VMEM((3, D, D), bf16), pltpu.VMEM((2, D, PAIR), bf16),
            pltpu.SemaphoreType.DMA((3,)), pltpu.SemaphoreType.DMA((2,)), pltpu.SemaphoreType.DMA((2,)),
        ],
    )(sc, tokens, q, k, v, pre, init, cos, sin, table, w_out, w_up, w_down, gains, biases, cot)


def sigmoid_of(soft):
    return jnp.where(soft < 0.01, soft * (1.0 - 0.5 * soft), 1.0 - jnp.exp(-soft))


def attend_back_kernel(
    angle, block, own, sc, tok, q_ref, k_ref, v_ref, dnum_ref, dden_ref, pre, init, part, d_init, cos, sin, table, table_t,
    *refs,
):
    if own:
        *got, out_ref, keep_ref, send_ref, run, acc, wide = refs
    else:
        out_ref, *other_refs, run, acc = refs
    pairs = PAIRS // 2
    later = sc[0].astype(f32)

    @pl.when(pl.program_id(0) == 0)
    def _():
        for p in range(pairs):
            run[p] = turn_state(d_init[p], -angle, 1.0 - later)

    second = lane_head(CHUNK) == 1
    second2 = jnp.concatenate([second, second], axis=1)

    for p in range(pairs):
        cols = slice(p * PAIR, (p + 1) * PAIR)
        q, k, v = q_ref[:, cols], k_ref[:, cols], v_ref[:, cols]
        q_wide, k_wide = q.astype(f32), k.astype(f32)
        dnum = dnum_ref[:, cols]
        grad = jnp.concatenate([dnum, dden_ref[:, cols]], axis=1)
        v_ones = with_ones(v)
        state = unpack_state(pre[0, p] + turn_state(init[p], angle, later))
        d_state = unpack_state(run[p])
        run[p] += part[0, p]
        dq_feat = nt(grad, state)
        dk_feat = nt(v_ones, d_state)
        dv = nn(features(k_wide, cos[...], sin[...]), d_state[:, :PAIR])
        dq = dq_feat[:, :PAIR] * cos[...] + dq_feat[:, PAIR:] * sin[...]
        dk = dk_feat[:, :PAIR] * cos[...] + dk_feat[:, PAIR:] * sin[...]
        q_apart, k_apart = heads_apart(q, second), heads_apart(k, second)
        d_scores = (nt(grad, heads_apart(v_ones, second2)) * table[...]).astype(bf16)
        dq += nn(d_scores, k_apart)
        scores_t = (nt(k, q_apart) * table_t[...]).astype(bf16)
        d_scores_t = (nt(v_ones, heads_apart(grad, second2)) * table_t[...]).astype(bf16)
        dk += nn(d_scores_t, q_apart)
        dv += nn(scores_t, heads_apart(dnum, second))
        out_ref[:, cols] = (dq.astype(bf16).astype(f32) * sigmoid_of(q_wide)).astype(bf16)
        out_ref[:, slice(HALF + p * PAIR, HALF + (p + 1) * PAIR)] = (
            dk.astype(bf16).astype(f32) * sigmoid_of(k_wide)
        ).astype(bf16)
        out_ref[:, slice(D + p * PAIR, D + (p + 1) * PAIR)] = dv.astype(bf16)
    acc[...] = jnp.where(pl.program_id(0) == 0, 0.0, acc[...]) + tn(tok[...], out_ref[...])

    @pl.when(pl.program_id(0) == pl.num_programs(0) - 1)
    def _():
        me = sc[1] if own else sc[2]
        for b in range(D // block):
            to = pl.ds(pl.multiple_of((jnp.int32(b) ^ me) * block, block), block)
            for j in range(3):
                cols = slice(j * HALF, (j + 1) * HALF)
                piece = acc[b * block : (b + 1) * block, cols]
                if own:
                    wide[to, cols] = (piece + got[j][to, :].astype(f32)).astype(bf16)
                else:
                    other_refs[j][to, :] = piece.astype(bf16)
        if own:
            keep_ref[...] = wide[:HALF]
            send_ref[...] = wide[HALF:]


def attend_back(
    sc, tokens, q, k, v, dnum, dden, pre, init, part, d_init, cos, sin, table, table_t, block, got=None, deps=()
):
    own = got is not None
    rows = q.shape[0]
    steps = rows // CHUNK
    last = steps - 1
    pairs = PAIRS // 2

    def half(sc):
        return sc[0] if own else 1 - sc[0]

    def make(height):
        return jax.ShapeDtypeStruct((height, 3 * HALF), bf16)

    chunk = pl.BlockSpec((CHUNK, HALF), lambda i, sc: (last - i, half(sc)))
    states = pl.BlockSpec((1, pairs, FEAT, PAIR), lambda i, sc: (last - i, half(sc), 0, 0))
    state = pl.BlockSpec((pairs, FEAT, PAIR), lambda i, sc: (half(sc), 0, 0))
    thin = by_chunk(PAIR, last)
    return ordered_call(
        functools.partial(attend_back_kernel, STEP_ANGLE * rows, block, own),
        "attend_back",
        scalars=1,
        deps=deps,
        grid=(steps,),
        in_specs=[
            by_chunk(D, last), chunk, chunk, chunk, chunk, chunk, states, state, states, state, thin, thin,
            whole(CHUNK, 2 * CHUNK), whole(CHUNK, 2 * CHUNK),
        ] + [whole(D, HALF)] * (3 * own),
        out_specs=[by_chunk(3 * HALF, last)] + ([whole(HALF, 3 * HALF)] * 2 if own else [whole(D, HALF)] * 3),
        out_shape=[make(rows)] + ([make(HALF)] * 2 if own else [jax.ShapeDtypeStruct((D, HALF), bf16)] * 3),
        scratch_shapes=[pltpu.VMEM((pairs, FEAT, PAIR), f32), pltpu.VMEM((D, 3 * HALF), f32)]
        + [pltpu.VMEM((D, 3 * HALF), bf16)] * own,
    )(sc, tokens, q, k, v, dnum, dden, pre, init, part, d_init, cos, sin, table, table_t, *(got or ()))


def token_grad_kernel(sc, dres_one, first, second, wq1, wk1, wv1, wq2, wk2, wv2, out):
    total = dres_one[...]
    for d, weights in ((first, (wq1, wk1, wv1)), (second, (wq2, wk2, wv2))):
        for j, w in enumerate(weights):
            total += nt(d[:, j * HALF : (j + 1) * HALF], w[...])
    out[...] = total


def token_grad(sc, dres_one, other, own, wq, wk, wv, deps=()):
    rows = own.shape[0]
    w_other = pl.BlockSpec((D, HALF), lambda i, sc: (0, 1 - sc[0]))
    w_own = pl.BlockSpec((D, HALF), lambda i, sc: (0, sc[0]))
    return ordered_call(
        token_grad_kernel,
        "token_grad",
        scalars=1,
        deps=deps,
        grid=(rows // CHUNK,),
        in_specs=[by_chunk(D), by_chunk(3 * HALF), by_chunk(3 * HALF)] + [w_other] * 3 + [w_own] * 3,
        out_specs=by_chunk(D),
        out_shape=jax.ShapeDtypeStruct((rows, D), f32),
    )(sc, dres_one, other, own, wq, wk, wv, wq, wk, wv)


def small_call(kernel, ins, out_rows, name, deps=()):
    width = ins[0].shape[1]
    many = isinstance(out_rows, (list, tuple))

    def shape(rows):
        return jax.ShapeDtypeStruct((rows, width), bf16)

    return ordered_call(
        kernel,
        name,
        deps=deps,
        grid=(1,),
        in_specs=[whole(*x.shape) for x in ins],
        out_specs=[whole(r, width) for r in out_rows] if many else whole(out_rows, width),
        out_shape=[shape(r) for r in out_rows] if many else shape(out_rows),
    )(*ins)


def add_cut_kernel(a, b, *outs):
    rows = outs[0].shape[0]
    for i, out in enumerate(outs):
        at = slice(i * rows, (i + 1) * rows)
        out[...] = (a[at].astype(f32) + b[at].astype(f32)).astype(bf16)


def add_cut_parts_kernel(a, first, second, rest, keep, send):
    start = 0
    for part in (first, second, rest):
        cols = slice(start, start + part.shape[1])
        keep[:, cols] = (a[:HALF, cols].astype(f32) + part[:HALF].astype(f32)).astype(bf16)
        send[:, cols] = (a[HALF:, cols].astype(f32) + part[HALF:].astype(f32)).astype(bf16)
        start += part.shape[1]


def add_all_kernel(*refs):
    total = refs[0][...].astype(f32)
    for ref in refs[1:-1]:
        total += ref[...].astype(f32)
    refs[-1][...] = total.astype(bf16)


def join_kernel(*refs):
    rows = refs[0].shape[0]
    for i, ref in enumerate(refs[:-1]):
        refs[-1][i * rows : (i + 1) * rows] = ref[...]


def add_cut(a, b, parts, deps=()):
    return small_call(add_cut_kernel, [a, b], [a.shape[0] // parts] * parts, "add_cut", deps)


def add_all(parts, deps=()):
    return small_call(add_all_kernel, parts, parts[0].shape[0], "add_all", deps)


def join(parts, deps=()):
    return small_call(join_kernel, parts, len(parts) * parts[0].shape[0], "join", deps)


def restore(me, block, quarters, put, along_z=False):
    count = QUARTER // block
    for i, ref in enumerate(quarters):
        for j in range(count):
            place = j * len(quarters) + i if along_z else i * count + j
            put(
                pl.multiple_of((jnp.int32(place) ^ me) * block, block),
                ref[j * block : (j + 1) * block, :].astype(f32),
            )


def gather_kernel(block, by_rows, sc, *refs):
    mine, other, out = refs[:4], refs[4:8], refs[8]
    own_me, other_me = (sc[3], sc[4]) if by_rows else (sc[1], sc[2])

    def put(row, piece):
        out[pl.ds(row, block), :] = piece

    is_mine = pl.program_id(0) // 2 == sc[0]

    @pl.when(is_mine)
    def _():
        restore(own_me, block, mine, put, by_rows)

    @pl.when(jnp.logical_not(is_mine))
    def _():
        restore(other_me, block, other, put, by_rows)


def gather_units(sc, parts, block, by_rows, deps=()):
    def at(own):
        def index(g, sc):
            return (0, jnp.clip(g - 2 * (sc[0] if own else 1 - sc[0]), 0, 1))

        return pl.BlockSpec((QUARTER, D), index)

    return ordered_call(
        functools.partial(gather_kernel, block, by_rows),
        "gather_units",
        scalars=1,
        deps=deps,
        grid=(4,),
        in_specs=[at(True)] * 4 + [at(False)] * 4,
        out_specs=pl.BlockSpec((D, D), (lambda g, sc: (g, 0)) if by_rows else (lambda g, sc: (0, g))),
        out_shape=jax.ShapeDtypeStruct((4 * D, D) if by_rows else (D, 4 * D), f32),
    )(sc, *parts)


def half_of(block, sc, group, start, size, store):
    mine, other = group[:4], group[4:]

    def cut(refs):
        return [ref.at[:, start : start + size] for ref in refs]

    is_mine = pl.program_id(0) == sc[0]

    @pl.when(is_mine)
    def _():
        restore(sc[1], block, cut(mine), store)

    @pl.when(jnp.logical_not(is_mine))
    def _():
        restore(sc[2], block, cut(other), store)


def gather_qkv_kernel(block, sc, *refs):
    for j, out in enumerate(refs[8:]):
        def put(row, piece, out=out):
            out[pl.ds(row, block), :] = piece

        half_of(block, sc, refs[:8], j * HALF, HALF, put)


def gather_qkv(sc, parts, block, deps=()):
    shape = jax.ShapeDtypeStruct((D, D), f32)
    return ordered_call(
        functools.partial(gather_qkv_kernel, block),
        "gather_qkv",
        scalars=1,
        deps=deps,
        grid=(2,),
        in_specs=[whole(QUARTER, 3 * HALF)] * 8,
        out_specs=[pl.BlockSpec((D, HALF), lambda g, sc: (0, g))] * 3,
        out_shape=[shape] * 3,
    )(sc, *parts)


def gather_rest_kernel(block, sc, *refs):
    group, out, gains, biases, rows = refs[:8], *refs[8:]

    def put(row, piece):
        out[pl.ds(row, block), :] = piece

    def put_norm(row, piece):
        rows[pl.ds(row, block), :] = piece

    half_of(block, sc, group, 0, HALF, put)

    @pl.when(pl.program_id(0) == 0)
    def _():
        half_of(block, sc, group, HALF, PAIR, put_norm)
        for i in range(2):
            for j in range(PAIRS):
                cols = slice(j * PAIR, (j + 1) * PAIR)
                first, second = 2 * i * PAIRS + j, (2 * i + 1) * PAIRS + j
                gains[i : i + 1, cols] = rows[first : first + 1, :]
                biases[i : i + 1, cols] = rows[second : second + 1, :]


def gather_rest(sc, parts, block, deps=()):
    norm = jax.ShapeDtypeStruct((2, D), f32)
    spec = pl.BlockSpec((QUARTER, HALF + PAIR), lambda g, sc: (0, 2 * D // (HALF + PAIR)))
    return ordered_call(
        functools.partial(gather_rest_kernel, block),
        "gather_rest",
        scalars=1,
        deps=deps,
        grid=(2,),
        in_specs=[spec] * 8,
        out_specs=[pl.BlockSpec((D, HALF), lambda g, sc: (0, g)), whole(2, D), whole(2, D)],
        out_shape=[jax.ShapeDtypeStruct((D, D), f32), norm, norm],
        scratch_shapes=[pltpu.VMEM((D, PAIR), f32)],
    )(sc, *parts)


def make_local(n_dp, n_head):
    n_z = n_dp // 2
    direct = n_z == 4
    places = 4 if direct else 1
    block = QUARTER // places
    both_axes = ("dp", "head")

    def swap(x, partner):
        pairs = []
        for d in range(n_dp):
            for h in range(n_head):
                to_d, to_h = partner(d, h)
                pairs.append((d * n_head + h, to_d * n_head + to_h))
        return lax.ppermute(x, both_axes, pairs)

    def swap_core(x):
        return swap(x, lambda d, h: (d, h ^ 1))

    def swap_first(x):
        return swap(x, lambda d, h: (d ^ 1, h) if h % 2 else (d, h ^ 2))

    def swap_second(x):
        return swap(x, lambda d, h: (d, h ^ 2) if h % 2 else (d ^ 1, h))

    def swap_z(x, k):
        return swap(x, lambda d, h: (d ^ (2 * k), h))

    def sum_z(keep, got):
        both = keep.astype(f32) + got.astype(f32)
        same_z = [[2 * i + j for i in range(n_z)] for j in range(2)]
        return lax.psum(both, "dp", axis_index_groups=same_z).astype(bf16)

    def cut_z(keep, got, deps=()):
        parts = add_cut(keep, got, 4, deps)
        return [parts[0], swap_z(parts[1], 2), swap_z(parts[2], 1), swap_z(parts[3], 3)]

    def share_z(parts, deps=(), neighbours=False):
        share = add_all(parts, deps)
        near, far = swap_z(share, 1), swap_z(share, 2)
        return [share, far, near, swap_z(far, 1) if neighbours else swap_z(share, 3)]

    def step(pair, swap_next, deps=()):
        keep, send = add_cut(*pair, 2, deps)
        return [keep, swap_next(send)]

    def swap_near(x):
        return swap_z(x, 1)

    def swap_far(x):
        return swap_z(x, 2)

    def spread(parts, deps=()):
        own = join(parts, deps) if direct else parts[0]
        second = swap_second(own)
        first = swap_first(own)
        both = swap_first(second)
        quarters = [own, second, first, both]
        return quarters + [swap_core(x) for x in quarters]

    def local(tokens, w_query, w_key, w_value, w_out, w_up, w_down, norm_gains, norm_biases, cotangent):
        rows = tokens.shape[0]
        assert LENGTH == 2 * rows and n_head % 4 == 0 and n_dp % 2 == 0
        head, dp = lax.axis_index("head"), lax.axis_index("dp")
        core, x, y, z = head % 2, head // 2, dp % 2, dp // 2
        rank = z % 2 * 2 + z // 2 if direct else 0
        by_x, by_y = (2 * x + y) * places + rank, (2 * y + x) * places + rank
        z_x, z_y = (rank * 4 + 2 * x + y, rank * 4 + 2 * y + x) if direct else (by_x, by_y)
        sc = jnp.stack([core, *(jnp.where(core == 0, *pair) for pair in ((by_x, by_y), (by_y, by_x), (z_x, z_y), (z_y, z_x)))])
        sc = sc.astype(jnp.int32)
        angle = STEP_ANGLE * np.arange(rows)
        cos = jnp.asarray(np.broadcast_to(np.cos(angle)[:, None], (rows, PAIR)), f32)
        sin = jnp.asarray(np.broadcast_to(np.sin(angle)[:, None], (rows, PAIR)), f32)
        gap = np.arange(CHUNK)[:, None] - np.arange(CHUNK)[None, :]
        weights = np.where(gap >= 0, np.cos(STEP_ANGLE * gap), 0.0)
        table, table_t = (jnp.asarray(np.concatenate([w, w], axis=1), f32) for w in (weights, weights.T))

        q, k, v, pre, total = project(tokens, w_query, w_key, w_value, cos, sin)
        init = swap_core(total)
        out, dres_one, dnum, dden, part, d_total, one_own, one_other, two_own, *two_other = rows_call(
            sc, tokens, q, k, v, pre, init, cos, sin, table, w_out, w_up, w_down, norm_gains, norm_biases, cotangent, block
        )
        one_got = swap_core(one_other)
        d_init = swap_core(d_total)
        two_got = [swap_core(x) for x in two_other]
        along = (swap_near, swap_far, swap_first, swap_second) if direct else (swap_first, swap_second)
        one = step([one_own, one_got], along[0])
        two_keep, two_send = small_call(
            add_cut_parts_kernel, [two_own, *two_got], [HALF, HALF], "add_cut", deps=(one[0],)
        )
        two = [two_keep, swap_first(two_send)]
        att = functools.partial(
            attend_back, sc, tokens, q, k, v, dnum, dden, pre, init, part, d_init, cos, sin, table, table_t, block
        )
        d_other, *three_other = att(deps=(two_keep,))
        three_got = [swap_core(x) for x in three_other]
        one = step(one, along[1], deps=(d_other,))
        two = step(two, swap_second, deps=(one[0],))
        d_own, three_keep, three_send = att(three_got, deps=(two[0],))
        three = [three_keep, swap_first(three_send)]
        if direct:
            one = step(one, swap_first, deps=(three_keep,))
            two = step(two, swap_near, deps=(one[0],))
            one = step(one, swap_second, deps=(two[0],))
            three = step(three, swap_second, deps=(one[0],))
            two = step(two, swap_far, deps=(three[0],))
            one = share_z(one, deps=(two[0],))
            three = cut_z(*three, deps=(one[0],))
            two = share_z(two, deps=(three[0],), neighbours=True)
            one = spread(one, deps=(two[0],))
            three = share_z(three, deps=(one[0],))
            two = spread(two, deps=(three[0],))
        else:
            three = step(three, swap_second)
            one, two, three = spread([sum_z(*one)]), spread([sum_z(*two)]), [sum_z(*three)]
        d_tokens = token_grad(sc, dres_one, d_other, d_own, w_query, w_key, w_value, deps=(two[0],))
        three = spread(three, deps=(d_tokens,))
        grad_down = gather_units(sc, one, block, True, deps=(three[0],))
        grad_up = gather_units(sc, two, block, False, deps=(grad_down,))
        grad_out, grad_gains, grad_biases = gather_rest(sc, two, block, deps=(grad_up,))
        grad_qkv = gather_qkv(sc, three, block, deps=(grad_out,))
        return out, d_tokens, *grad_qkv, grad_out, grad_up, grad_down, grad_gains, grad_biases

    return local


def solution(mesh):
    rows, same = P(("dp", "head"), None), P()
    return jax.shard_map(
        make_local(mesh.shape["dp"], mesh.shape["head"]),
        mesh=mesh,
        in_specs=(rows,) + (same,) * 8 + (rows,),
        out_specs=(rows, rows) + (same,) * 8,
        check_vma=False,
    )
```

```python
import functools
import math

import jax
import jax.numpy as jnp
import numpy as np
from jax import lax
from jax.experimental import pallas as pl
from jax.experimental.pallas import tpu as pltpu
from jax.sharding import PartitionSpec as P

D = 768
E = 64
FF = 3072
LENGTH = 2048
CHUNK = 256
PAIR = 2 * E
PAIRS = D // PAIR
FEAT = 2 * PAIR
EPSILON = 1e-05
STEP_ANGLE = 0.5 * math.pi / LENGTH
HALF = D // 2
QUARTER = D // 4
LIMIT = 63 * 2**20
PACE = 1.0
WEIGHTS = dict(
    project=11, rows=60, attend_back=19, token_grad=10, gather_units=8, gather_qkv=5.5, gather_two=12, add_cut=2.5, add_all=2, join=2
)

f32 = jnp.float32
bf16 = jnp.bfloat16


def nn(a, b):
    return jnp.dot(a, b, preferred_element_type=f32)


def tn(a, b):
    return lax.dot_general(a, b, (((0,), (0,)), ((), ())), preferred_element_type=f32)


def nt(a, b):
    return lax.dot_general(a, b, (((1,), (1,)), ((), ())), preferred_element_type=f32)


def ordered_call(
    kernel, name, grid, in_specs, out_specs, out_shape, scratch_shapes=(), scalars=0, deps=(),
):
    deps = list(deps)

    def body(*refs):
        first = scalars + len(in_specs)
        kernel(*refs[:first], *refs[first + len(deps) :])

    call = pl.pallas_call(
        body,
        grid_spec=pltpu.PrefetchScalarGridSpec(
            num_scalar_prefetch=scalars,
            grid=grid,
            in_specs=list(in_specs) + [pl.BlockSpec(memory_space=pl.ANY)] * len(deps),
            out_specs=out_specs,
            scratch_shapes=list(scratch_shapes),
        ),
        out_shape=out_shape,
        compiler_params=pltpu.CompilerParams(vmem_limit_bytes=LIMIT),
        cost_estimate=pl.CostEstimate(
            flops=int(PACE * WEIGHTS[name] * 1.15e9) + 1, bytes_accessed=1, transcendentals=0
        ),
        name=name,
    )
    return lambda *args: call(*args, *deps)


def whole(*shape):
    return pl.BlockSpec(shape, lambda *_: (0,) * len(shape))


def by_chunk(width, last=None):
    if last is None:
        return pl.BlockSpec((CHUNK, width), lambda i, *_: (i, 0))
    return pl.BlockSpec((CHUNK, width), lambda i, *_: (last - i, 0))


ANY = pl.BlockSpec(memory_space=pl.ANY)


def softplus(x):
    return jnp.maximum(x, 0.0) + jnp.log1p(jnp.exp(-jnp.abs(x)))


def lane_head(rows):
    return (lax.broadcasted_iota(jnp.int32, (rows, PAIR), 1) >= E).astype(jnp.int32)


def row_head():
    return (lax.broadcasted_iota(jnp.int32, (FEAT, PAIR), 0) % PAIR >= E).astype(jnp.int32)


def unpack_state(packed):
    same = row_head() == lane_head(FEAT)
    left = jnp.where(same, packed, 0.0)
    right = jnp.where(same, pltpu.roll(packed, E, 1), 0.0)
    return jnp.concatenate([left, right], axis=1).astype(bf16)


def features(x, cosine, sine):
    return jnp.concatenate([x * cosine, x * sine], axis=1).astype(bf16)


def with_ones(v):
    return jnp.concatenate([v, jnp.ones_like(v)], axis=1)


def heads_apart(x, second):
    zero = jnp.zeros_like(x)
    return jnp.concatenate([jnp.where(second, zero, x), jnp.where(second, x, zero)], axis=0)


def turn_state(state, angle, on):
    cosine, sine = math.cos(angle) * on, math.sin(angle) * on
    first, second = state[:PAIR], state[PAIR:]
    return jnp.concatenate([cosine * first + sine * second, cosine * second - sine * first], axis=0)


def project_kernel(tok, wq, wk, wv, cos, sin, q_ref, k_ref, v_ref, pre_ref, tot_ref):
    @pl.when(pl.program_id(0) == 0)
    def _():
        tot_ref[...] = jnp.zeros_like(tot_ref)

    x = tok[...]
    q_ref[...] = softplus(nn(x, wq[...])).astype(bf16)
    k = softplus(nn(x, wk[...])).astype(bf16)
    k_ref[...] = k
    v = nn(x, wv[...]).astype(bf16)
    v_ref[...] = v
    same = row_head() == lane_head(FEAT)
    for p in range(PAIRS):
        cols = slice(p * PAIR, (p + 1) * PAIR)
        k_feat = features(k[:, cols].astype(f32), cos[...], sin[...])
        both = tn(k_feat, with_ones(v[:, cols]))
        pre_ref[0, p] = tot_ref[p]
        tot_ref[p] += jnp.where(same, both[:, :PAIR], both[:, PAIR:])


def project(tokens, wq, wk, wv, cos, sin):
    rows = tokens.shape[0]
    steps = rows // CHUNK
    act = jax.ShapeDtypeStruct((rows, D), bf16)
    return ordered_call(
        project_kernel,
        "project",
        grid=(steps,),
        in_specs=[by_chunk(D), whole(D, D), whole(D, D), whole(D, D), by_chunk(PAIR), by_chunk(PAIR)],
        out_specs=[
            by_chunk(D), by_chunk(D), by_chunk(D),
            pl.BlockSpec((1, PAIRS, FEAT, PAIR), lambda i: (i, 0, 0, 0)), whole(PAIRS, FEAT, PAIR),
        ],
        out_shape=[
            act, act, act,
            jax.ShapeDtypeStruct((steps, PAIRS, FEAT, PAIR), f32), jax.ShapeDtypeStruct((PAIRS, FEAT, PAIR), f32),
        ],
    )(tokens, wq, wk, wv, cos, sin)


def norm_parts(z):
    centred = z - jnp.mean(z, axis=-1, keepdims=True)
    rstd = lax.rsqrt(jnp.mean(centred * centred, axis=-1, keepdims=True) + EPSILON)
    return centred * rstd, rstd


def norm_back(t, n, rstd):
    return (t - jnp.mean(t, axis=-1, keepdims=True) - n * jnp.mean(t * n, axis=-1, keepdims=True)) * rstd


def rows_kernel(
    angle, block, sc, tok, q_ref, k_ref, v_ref, pre, init, cos, sin, table, w_out, w_up_hbm, w_down_hbm, gains, biases, cot,
    out_ref, dres_one_ref, dnum_ref, dden_ref, part_ref, tot_ref, one_own, one_other, two_own, two_first, two_second, two_rest,
    w_up, w_down, mixed, hid, slope, dhid, acc_down, acc_up, acc_out, ng, stage, norm_stage, sems, norm_sems, w_sems,
):
    core = sc[0]
    step = pl.program_id(0)
    first = step == 0

    def weight_copies():
        return (
            pltpu.make_async_copy(w_up_hbm, w_up, w_sems.at[0]),
            pltpu.make_async_copy(w_down_hbm, w_down, w_sems.at[1]),
        )

    @pl.when(first)
    def _():
        for copy in weight_copies():
            copy.start()
        ng[...] = jnp.zeros_like(ng)
        tot_ref[...] = jnp.zeros_like(tot_ref)

    later = core.astype(f32)
    second = lane_head(CHUNK) == 1
    second2 = jnp.concatenate([second, second], axis=1)
    inverse = []
    for p in range(PAIRS):
        cols = slice(p * PAIR, (p + 1) * PAIR)
        state = unpack_state(pre[0, p] + turn_state(init[p], angle, later))
        q, k, v = q_ref[:, cols], k_ref[:, cols], v_ref[:, cols]
        total = nn(features(q.astype(f32), cos[...], sin[...]), state)
        scores = (nt(q, heads_apart(k, second)) * table[...]).astype(bf16)
        total += nn(scores, heads_apart(with_ones(v), second2))
        inv = 1.0 / total[:, PAIR:]
        inverse.append(inv)
        mixed[:, cols] = (total[:, :PAIR] * inv).astype(bf16)
    z = tok[...].astype(f32) + nn(mixed[...], w_out[...])
    n0, rstd0 = norm_parts(z)
    normed = n0 * gains[0:1] + biases[0:1]
    low = normed.astype(bf16)

    @pl.when(first)
    def _():
        for copy in weight_copies():
            copy.wait()

    for j in range(FF // D):
        cols = slice(j * D, (j + 1) * D)
        h = nn(low, w_up[:, cols])
        phi = 0.5 * (1.0 + lax.erf(h * (0.5**0.5)))
        hid[:, cols] = (h * phi).astype(bf16)
        slope[:, cols] = phi + h * jnp.exp(-0.5 * h * h) * ((2 * math.pi) ** -0.5)
    z = normed + nn(hid[...], w_down[...])
    n1, rstd1 = norm_parts(z)
    out_ref[...] = (n1 * gains[1:2] + biases[1:2]).astype(bf16)
    g = cot[...].astype(f32)
    ng[2:3] += jnp.sum(g * n1, axis=0, keepdims=True)
    ng[3:4] += jnp.sum(g, axis=0, keepdims=True)
    dres = norm_back(g * gains[1:2], n1, rstd1)
    dffn = dres.astype(bf16)
    for j in range(FF // D):
        cols = slice(j * D, (j + 1) * D)
        dhid[:, cols] = (nt(dffn, w_down[cols, :]) * slope[:, cols]).astype(bf16)
    g = dres + nt(dhid[...], w_up[...])
    ng[0:1] += jnp.sum(g * n0, axis=0, keepdims=True)
    ng[1:2] += jnp.sum(g, axis=0, keepdims=True)
    dres_one = norm_back(g * gains[0:1], n0, rstd0)
    dres_one_ref[...] = dres_one
    dbranch = dres_one.astype(bf16)
    dmixed = nt(dbranch, w_out[...]).astype(bf16).astype(f32)
    lane = lax.broadcasted_iota(jnp.int32, (CHUNK, PAIR), 1)
    same = row_head() == lane_head(FEAT)
    for p in range(PAIRS):
        cols = slice(p * PAIR, (p + 1) * PAIR)
        dnum = (dmixed[:, cols] * inverse[p]).astype(bf16)
        dnum_ref[:, cols] = dnum
        moment = dnum.astype(f32) * mixed[:, cols].astype(f32)
        first_sum = jnp.sum(jnp.where(second, 0.0, moment), axis=1, keepdims=True)
        second_sum = jnp.sum(jnp.where(second, moment, 0.0), axis=1, keepdims=True)
        dden = jnp.where(second, second_sum, first_sum) * (-2.0 / E)
        high = dden.astype(bf16)
        rest = (dden - high.astype(f32)).astype(bf16)
        dden = jnp.where(lane % E < E // 2, high, rest)
        dden_ref[:, cols] = dden
        both = tn(features(q_ref[:, cols].astype(f32), cos[...], sin[...]), jnp.concatenate([dnum, dden], axis=1))
        part = jnp.where(same, both[:, :PAIR], pltpu.roll(both[:, PAIR:], E, 1))
        part_ref[0, p] = part
        tot_ref[p] += part
    for j in range(FF // D):
        cols = slice(j * D, (j + 1) * D)
        acc_down[cols, :] = jnp.where(first, 0.0, acc_down[cols, :]) + tn(hid[:, cols], dffn)
        acc_up[:, cols] = jnp.where(first, 0.0, acc_up[:, cols]) + tn(low, dhid[:, cols])
    acc_out[...] = jnp.where(first, 0.0, acc_out[...]) + tn(mixed[...], dbranch)

    @pl.when(step == pl.num_programs(0) - 1)
    def _():
        slots = stage.shape[0]
        jobs = []
        for j in range(4):
            jobs.append((acc_down.at[j * D : (j + 1) * D, :], j // 2, one_own, one_other, j % 2 * D, j % 2 * D, D))
        for j in range(4):
            jobs.append((acc_up.at[:, j * D : (j + 1) * D], j // 2, two_own, two_second if j % 2 else two_first, j % 2 * D, 0, D))
        for j in range(2):
            jobs.append((acc_out.at[:, j * HALF : (j + 1) * HALF], j, two_own, two_rest, 2 * D, 0, HALF))

        def move(i, do):
            _, owner, own, other, own_at, other_at, size = jobs[i]
            slot = i % slots

            def one(to, start):
                do(pltpu.make_async_copy(stage.at[slot, :, pl.ds(0, size)], to.at[:, pl.ds(start, size)], sems.at[slot]))

            @pl.when(core == owner)
            def _():
                one(own, own_at)

            @pl.when(core != owner)
            def _():
                one(other, other_at)

        for i, (acc, owner, _, _, _, _, size) in enumerate(jobs):
            if i >= slots:
                move(i - slots, lambda copy: copy.wait())
            me = jnp.where(core == owner, sc[3 if i < 4 else 1], sc[4 if i < 4 else 2])
            for b in range(D // block):
                to = pl.multiple_of((jnp.int32(b) ^ me) * block, block)
                stage[i % slots, pl.ds(to, block), :size] = acc[b * block : (b + 1) * block, :].astype(bf16)
            move(i, lambda copy: copy.start())
        norm_stage[...] = jnp.zeros_like(norm_stage)
        copies = []
        for i, (me, to, start) in enumerate(((sc[1], two_own, 2 * D + HALF), (sc[2], two_rest, HALF))):
            base = pl.multiple_of(me * block, block)
            rows = [ng[r : r + 1, j * PAIR : (j + 1) * PAIR] for r in range(4) for j in range(PAIRS)]
            rows.append(jnp.zeros((block - len(rows), PAIR), f32))
            norm_stage[i, pl.ds(base, block), :] = jnp.concatenate(rows, axis=0).astype(bf16)
            copy = pltpu.make_async_copy(norm_stage.at[i], to.at[:, pl.ds(start, PAIR)], norm_sems.at[i])
            copy.start()
            copies.append(copy)
        for i in range(len(jobs) - slots, len(jobs)):
            move(i, lambda copy: copy.wait())
        for copy in copies:
            copy.wait()


def rows_call(sc, tokens, q, k, v, pre, init, cos, sin, table, w_out, w_up, w_down, gains, biases, cot, block):
    rows = tokens.shape[0]
    steps = rows // CHUNK

    def make(width, dtype=bf16, height=rows):
        return jax.ShapeDtypeStruct((height, width), dtype)

    def once(*shape):
        return pl.BlockSpec(shape, lambda *_: (0,) * len(shape), pipeline_mode=pl.Buffered(1))

    chunk, thin = by_chunk(D), by_chunk(PAIR)
    states = pl.BlockSpec((1, PAIRS, FEAT, PAIR), lambda i, sc: (i, 0, 0, 0))
    one, two = 2 * D, 2 * D + HALF + PAIR
    return ordered_call(
        functools.partial(rows_kernel, STEP_ANGLE * rows, block),
        "rows",
        scalars=1,
        grid=(steps,),
        in_specs=[
            chunk, chunk, chunk, chunk, states, once(PAIRS, FEAT, PAIR), thin, thin, once(CHUNK, 2 * CHUNK),
            once(D, D), ANY, ANY, once(2, D), once(2, D), chunk,
        ],
        out_specs=[chunk, chunk, chunk, chunk, states, whole(PAIRS, FEAT, PAIR)] + [ANY] * 6,
        out_shape=[
            make(D), make(D, f32), make(D), make(D), jax.ShapeDtypeStruct((steps, PAIRS, FEAT, PAIR), f32),
            jax.ShapeDtypeStruct((PAIRS, FEAT, PAIR), f32),
            make(one, bf16, D), make(one, bf16, D), make(two, bf16, D), make(D, bf16, D), make(D, bf16, D),
            make(HALF + PAIR, bf16, D),
        ],
        scratch_shapes=[
            pltpu.VMEM((D, FF), bf16), pltpu.VMEM((FF, D), bf16),
            pltpu.VMEM((CHUNK, D), bf16), pltpu.VMEM((CHUNK, FF), bf16), pltpu.VMEM((CHUNK, FF), f32),
            pltpu.VMEM((CHUNK, FF), bf16), pltpu.VMEM((FF, D), f32), pltpu.VMEM((D, FF), f32), pltpu.VMEM((D, D), f32),
            pltpu.VMEM((4, D), f32), pltpu.VMEM((3, D, D), bf16), pltpu.VMEM((2, D, PAIR), bf16),
            pltpu.SemaphoreType.DMA((3,)), pltpu.SemaphoreType.DMA((2,)), pltpu.SemaphoreType.DMA((2,)),
        ],
    )(sc, tokens, q, k, v, pre, init, cos, sin, table, w_out, w_up, w_down, gains, biases, cot)


def sigmoid_of(soft):
    return jnp.where(soft < 0.01, soft * (1.0 - 0.5 * soft), 1.0 - jnp.exp(-soft))


def attend_back_kernel(
    angle, block, own, sc, tok, q_ref, k_ref, v_ref, dnum_ref, dden_ref, pre, init, part, d_init, cos, sin, table, table_t,
    *refs,
):
    if own:
        *got, out_ref, keep_ref, send_ref, run, acc, wide = refs
    else:
        out_ref, *other_refs, run, acc = refs
    pairs = PAIRS // 2
    later = sc[0].astype(f32)

    @pl.when(pl.program_id(0) == 0)
    def _():
        for p in range(pairs):
            run[p] = turn_state(d_init[p], -angle, 1.0 - later)

    second = lane_head(CHUNK) == 1
    second2 = jnp.concatenate([second, second], axis=1)

    for p in range(pairs):
        cols = slice(p * PAIR, (p + 1) * PAIR)
        q, k, v = q_ref[:, cols], k_ref[:, cols], v_ref[:, cols]
        q_wide, k_wide = q.astype(f32), k.astype(f32)
        dnum = dnum_ref[:, cols]
        grad = jnp.concatenate([dnum, dden_ref[:, cols]], axis=1)
        v_ones = with_ones(v)
        state = unpack_state(pre[0, p] + turn_state(init[p], angle, later))
        d_state = unpack_state(run[p])
        run[p] += part[0, p]
        dq_feat = nt(grad, state)
        dk_feat = nt(v_ones, d_state)
        dv = nn(features(k_wide, cos[...], sin[...]), d_state[:, :PAIR])
        dq = dq_feat[:, :PAIR] * cos[...] + dq_feat[:, PAIR:] * sin[...]
        dk = dk_feat[:, :PAIR] * cos[...] + dk_feat[:, PAIR:] * sin[...]
        q_apart, k_apart = heads_apart(q, second), heads_apart(k, second)
        d_scores = (nt(grad, heads_apart(v_ones, second2)) * table[...]).astype(bf16)
        dq += nn(d_scores, k_apart)
        scores_t = (nt(k, q_apart) * table_t[...]).astype(bf16)
        d_scores_t = (nt(v_ones, heads_apart(grad, second2)) * table_t[...]).astype(bf16)
        dk += nn(d_scores_t, q_apart)
        dv += nn(scores_t, heads_apart(dnum, second))
        out_ref[:, cols] = (dq.astype(bf16).astype(f32) * sigmoid_of(q_wide)).astype(bf16)
        out_ref[:, slice(HALF + p * PAIR, HALF + (p + 1) * PAIR)] = (
            dk.astype(bf16).astype(f32) * sigmoid_of(k_wide)
        ).astype(bf16)
        out_ref[:, slice(D + p * PAIR, D + (p + 1) * PAIR)] = dv.astype(bf16)
    acc[...] = jnp.where(pl.program_id(0) == 0, 0.0, acc[...]) + tn(tok[...], out_ref[...])

    @pl.when(pl.program_id(0) == pl.num_programs(0) - 1)
    def _():
        me = sc[1] if own else sc[2]
        for b in range(D // block):
            to = pl.ds(pl.multiple_of((jnp.int32(b) ^ me) * block, block), block)
            for j in range(3):
                cols = slice(j * HALF, (j + 1) * HALF)
                piece = acc[b * block : (b + 1) * block, cols]
                if own:
                    wide[to, cols] = (piece + got[j][to, :].astype(f32)).astype(bf16)
                else:
                    other_refs[j][to, :] = piece.astype(bf16)
        if own:
            keep_ref[...] = wide[:HALF]
            send_ref[...] = wide[HALF:]


def attend_back(
    sc, tokens, q, k, v, dnum, dden, pre, init, part, d_init, cos, sin, table, table_t, block, got=None, deps=()
):
    own = got is not None
    rows = q.shape[0]
    steps = rows // CHUNK
    last = steps - 1
    pairs = PAIRS // 2

    def half(sc):
        return sc[0] if own else 1 - sc[0]

    def make(height):
        return jax.ShapeDtypeStruct((height, 3 * HALF), bf16)

    chunk = pl.BlockSpec((CHUNK, HALF), lambda i, sc: (last - i, half(sc)))
    states = pl.BlockSpec((1, pairs, FEAT, PAIR), lambda i, sc: (last - i, half(sc), 0, 0))
    state = pl.BlockSpec((pairs, FEAT, PAIR), lambda i, sc: (half(sc), 0, 0))
    thin = by_chunk(PAIR, last)
    return ordered_call(
        functools.partial(attend_back_kernel, STEP_ANGLE * rows, block, own),
        "attend_back",
        scalars=1,
        deps=deps,
        grid=(steps,),
        in_specs=[
            by_chunk(D, last), chunk, chunk, chunk, chunk, chunk, states, state, states, state, thin, thin,
            whole(CHUNK, 2 * CHUNK), whole(CHUNK, 2 * CHUNK),
        ] + [whole(D, HALF)] * (3 * own),
        out_specs=[by_chunk(3 * HALF, last)] + ([whole(HALF, 3 * HALF)] * 2 if own else [whole(D, HALF)] * 3),
        out_shape=[make(rows)] + ([make(HALF)] * 2 if own else [jax.ShapeDtypeStruct((D, HALF), bf16)] * 3),
        scratch_shapes=[pltpu.VMEM((pairs, FEAT, PAIR), f32), pltpu.VMEM((D, 3 * HALF), f32)]
        + [pltpu.VMEM((D, 3 * HALF), bf16)] * own,
    )(sc, tokens, q, k, v, dnum, dden, pre, init, part, d_init, cos, sin, table, table_t, *(got or ()))


def token_grad_kernel(sc, dres_one, first, second, wq1, wk1, wv1, wq2, wk2, wv2, out):
    total = dres_one[...]
    for d, weights in ((first, (wq1, wk1, wv1)), (second, (wq2, wk2, wv2))):
        for j, w in enumerate(weights):
            total += nt(d[:, j * HALF : (j + 1) * HALF], w[...])
    out[...] = total


def token_grad(sc, dres_one, other, own, wq, wk, wv, deps=()):
    rows = own.shape[0]
    w_other = pl.BlockSpec((D, HALF), lambda i, sc: (0, 1 - sc[0]))
    w_own = pl.BlockSpec((D, HALF), lambda i, sc: (0, sc[0]))
    return ordered_call(
        token_grad_kernel,
        "token_grad",
        scalars=1,
        deps=deps,
        grid=(rows // CHUNK,),
        in_specs=[by_chunk(D), by_chunk(3 * HALF), by_chunk(3 * HALF)] + [w_other] * 3 + [w_own] * 3,
        out_specs=by_chunk(D),
        out_shape=jax.ShapeDtypeStruct((rows, D), f32),
    )(sc, dres_one, other, own, wq, wk, wv, wq, wk, wv)


def small_call(kernel, ins, out_rows, name, deps=()):
    width = ins[0].shape[1]
    many = isinstance(out_rows, (list, tuple))
    cuts = 2 if ins[0].shape[0] == D and all(x.shape == ins[0].shape for x in ins) else 1

    def spec(x_rows, x_width):
        return pl.BlockSpec((x_rows, x_width // cuts), lambda i: (0, i))

    def shape(rows):
        return jax.ShapeDtypeStruct((rows, width), bf16)

    return ordered_call(
        kernel,
        name,
        deps=deps,
        grid=(cuts,),
        in_specs=[spec(*x.shape) for x in ins],
        out_specs=[spec(r, width) for r in out_rows] if many else spec(out_rows, width),
        out_shape=[shape(r) for r in out_rows] if many else shape(out_rows),
    )(*ins)


def add_cut_kernel(a, b, *outs):
    rows = outs[0].shape[0]
    for i, out in enumerate(outs):
        at = slice(i * rows, (i + 1) * rows)
        out[...] = (a[at].astype(f32) + b[at].astype(f32)).astype(bf16)


def add_cut_parts_kernel(a, first, second, rest, keep, send):
    start = 0
    for part in (first, second, rest):
        cols = slice(start, start + part.shape[1])
        keep[:, cols] = (a[:HALF, cols].astype(f32) + part[:HALF].astype(f32)).astype(bf16)
        send[:, cols] = (a[HALF:, cols].astype(f32) + part[HALF:].astype(f32)).astype(bf16)
        start += part.shape[1]


def add_all_kernel(*refs):
    total = refs[0][...].astype(f32)
    for ref in refs[1:-1]:
        total += ref[...].astype(f32)
    refs[-1][...] = total.astype(bf16)


def join_kernel(*refs):
    rows = refs[0].shape[0]
    for i, ref in enumerate(refs[:-1]):
        refs[-1][i * rows : (i + 1) * rows] = ref[...]


def add_cut(a, b, parts, deps=()):
    return small_call(add_cut_kernel, [a, b], [a.shape[0] // parts] * parts, "add_cut", deps)


def add_all(parts, deps=()):
    return small_call(add_all_kernel, parts, parts[0].shape[0], "add_all", deps)


def join(parts, deps=()):
    return small_call(join_kernel, parts, len(parts) * parts[0].shape[0], "join", deps)


def restore(me, block, quarters, put, along_z=False):
    count = QUARTER // block
    for i, ref in enumerate(quarters):
        for j in range(count):
            place = j * len(quarters) + i if along_z else i * count + j
            put(
                pl.multiple_of((jnp.int32(place) ^ me) * block, block),
                ref[j * block : (j + 1) * block, :].astype(f32),
            )


def gather_kernel(block, by_rows, sc, *refs):
    mine, other, out = refs[:4], refs[4:8], refs[8]
    own_me, other_me = (sc[3], sc[4]) if by_rows else (sc[1], sc[2])

    def put(row, piece):
        out[pl.ds(row, block), :] = piece

    is_mine = pl.program_id(0) // 2 == sc[0]

    @pl.when(is_mine)
    def _():
        restore(own_me, block, mine, put, by_rows)

    @pl.when(jnp.logical_not(is_mine))
    def _():
        restore(other_me, block, other, put, by_rows)


def gather_units(sc, parts, block, by_rows, deps=()):
    def at(own):
        def index(g, sc):
            return (0, jnp.clip(g - 2 * (sc[0] if own else 1 - sc[0]), 0, 1))

        return pl.BlockSpec((QUARTER, D), index)

    return ordered_call(
        functools.partial(gather_kernel, block, by_rows),
        "gather_units",
        scalars=1,
        deps=deps,
        grid=(4,),
        in_specs=[at(True)] * 4 + [at(False)] * 4,
        out_specs=pl.BlockSpec((D, D), (lambda g, sc: (g, 0)) if by_rows else (lambda g, sc: (0, g))),
        out_shape=jax.ShapeDtypeStruct((4 * D, D) if by_rows else (D, 4 * D), f32),
    )(sc, *parts)


def half_of(block, sc, group, start, size, store):
    mine, other = group[:4], group[4:]

    def cut(refs):
        return [ref.at[:, start : start + size] for ref in refs]

    is_mine = pl.program_id(0) == sc[0]

    @pl.when(is_mine)
    def _():
        restore(sc[1], block, cut(mine), store)

    @pl.when(jnp.logical_not(is_mine))
    def _():
        restore(sc[2], block, cut(other), store)


def gather_qkv_kernel(block, sc, *refs):
    for j, out in enumerate(refs[8:]):
        def put(row, piece, out=out):
            out[pl.ds(row, block), :] = piece

        half_of(block, sc, refs[:8], j * HALF, HALF, put)


def gather_qkv(sc, parts, block, deps=()):
    shape = jax.ShapeDtypeStruct((D, D), f32)
    return ordered_call(
        functools.partial(gather_qkv_kernel, block),
        "gather_qkv",
        scalars=1,
        deps=deps,
        grid=(2,),
        in_specs=[whole(QUARTER, 3 * HALF)] * 8,
        out_specs=[pl.BlockSpec((D, HALF), lambda g, sc: (0, g))] * 3,
        out_shape=[shape] * 3,
    )(sc, *parts)


def gather_two_kernel(block, sc, *refs):
    units, group = (*refs[:8], refs[16]), refs[8:16]
    out, gains, biases, rows = refs[17:]
    step = pl.program_id(0)
    gather_kernel(block, False, sc, *units)

    def put(row, piece):
        out[pl.ds(row, block), :] = piece

    def put_norm(row, piece):
        rows[pl.ds(row, block), :] = piece

    @pl.when(step < 2)
    def _():
        half_of(block, sc, group, 0, HALF, put)

    @pl.when(step == 0)
    def _():
        half_of(block, sc, group, HALF, PAIR, put_norm)
        for i in range(2):
            for j in range(PAIRS):
                cols = slice(j * PAIR, (j + 1) * PAIR)
                first, second = 2 * i * PAIRS + j, (2 * i + 1) * PAIRS + j
                gains[i : i + 1, cols] = rows[first : first + 1, :]
                biases[i : i + 1, cols] = rows[second : second + 1, :]


def gather_two(sc, parts, block, deps=()):
    def at(own):
        def index(g, sc):
            return (0, jnp.clip(g - 2 * (sc[0] if own else 1 - sc[0]), 0, 1))

        return pl.BlockSpec((QUARTER, D), index)

    norm = jax.ShapeDtypeStruct((2, D), f32)
    rest = pl.BlockSpec((QUARTER, HALF + PAIR), lambda g, sc: (0, 2 * D // (HALF + PAIR)))
    return ordered_call(
        functools.partial(gather_two_kernel, block),
        "gather_two",
        scalars=1,
        deps=deps,
        grid=(4,),
        in_specs=[at(True)] * 4 + [at(False)] * 4 + [rest] * 8,
        out_specs=[
            pl.BlockSpec((D, D), lambda g, sc: (0, g)), pl.BlockSpec((D, HALF), lambda g, sc: (0, jnp.minimum(g, 1))),
            whole(2, D), whole(2, D),
        ],
        out_shape=[jax.ShapeDtypeStruct((D, 4 * D), f32), jax.ShapeDtypeStruct((D, D), f32), norm, norm],
        scratch_shapes=[pltpu.VMEM((D, PAIR), f32)],
    )(sc, *parts, *parts)


def make_local(n_dp, n_head):
    n_z = n_dp // 2
    direct = n_z == 4
    places = 4 if direct else 1
    block = QUARTER // places
    both_axes = ("dp", "head")

    def swap(x, partner):
        pairs = []
        for d in range(n_dp):
            for h in range(n_head):
                to_d, to_h = partner(d, h)
                pairs.append((d * n_head + h, to_d * n_head + to_h))
        return lax.ppermute(x, both_axes, pairs)

    def swap_core(x):
        return swap(x, lambda d, h: (d, h ^ 1))

    def swap_first(x):
        return swap(x, lambda d, h: (d ^ 1, h) if h % 2 else (d, h ^ 2))

    def swap_second(x):
        return swap(x, lambda d, h: (d, h ^ 2) if h % 2 else (d ^ 1, h))

    def swap_z(x, k):
        return swap(x, lambda d, h: (d ^ (2 * k), h))

    def sum_z(keep, got):
        both = keep.astype(f32) + got.astype(f32)
        same_z = [[2 * i + j for i in range(n_z)] for j in range(2)]
        return lax.psum(both, "dp", axis_index_groups=same_z).astype(bf16)

    def cut_z(keep, got, deps=()):
        parts = add_cut(keep, got, 4, deps)
        return [parts[0], swap_z(parts[1], 2), swap_z(parts[2], 1), swap_z(parts[3], 3)]

    def share_z(parts, deps=(), neighbours=False):
        share = add_all(parts, deps)
        near, far = swap_z(share, 1), swap_z(share, 2)
        return [share, far, near, swap_z(far, 1) if neighbours else swap_z(share, 3)]

    def step(pair, swap_next, deps=()):
        keep, send = add_cut(*pair, 2, deps)
        return [keep, swap_next(send)]

    def swap_near(x):
        return swap_z(x, 1)

    def swap_far(x):
        return swap_z(x, 2)

    def spread(parts, deps=()):
        own = join(parts, deps) if direct else parts[0]
        second = swap_second(own)
        first = swap_first(own)
        both = swap_first(second)
        quarters = [own, second, first, both]
        return quarters + [swap_core(x) for x in quarters]

    def local(tokens, w_query, w_key, w_value, w_out, w_up, w_down, norm_gains, norm_biases, cotangent):
        rows = tokens.shape[0]
        assert LENGTH == 2 * rows and n_head % 4 == 0 and n_dp % 2 == 0
        head, dp = lax.axis_index("head"), lax.axis_index("dp")
        core, x, y, z = head % 2, head // 2, dp % 2, dp // 2
        rank = z % 2 * 2 + z // 2 if direct else 0
        by_x, by_y = (2 * x + y) * places + rank, (2 * y + x) * places + rank
        z_x, z_y = (rank * 4 + 2 * x + y, rank * 4 + 2 * y + x) if direct else (by_x, by_y)
        sc = jnp.stack([core, *(jnp.where(core == 0, *pair) for pair in ((by_x, by_y), (by_y, by_x), (z_x, z_y), (z_y, z_x)))])
        sc = sc.astype(jnp.int32)
        angle = STEP_ANGLE * np.arange(rows)
        cos = jnp.asarray(np.broadcast_to(np.cos(angle)[:, None], (rows, PAIR)), f32)
        sin = jnp.asarray(np.broadcast_to(np.sin(angle)[:, None], (rows, PAIR)), f32)
        gap = np.arange(CHUNK)[:, None] - np.arange(CHUNK)[None, :]
        weights = np.where(gap >= 0, np.cos(STEP_ANGLE * gap), 0.0)
        table, table_t = (jnp.asarray(np.concatenate([w, w], axis=1), f32) for w in (weights, weights.T))

        q, k, v, pre, total = project(tokens, w_query, w_key, w_value, cos, sin)
        init = swap_core(total)
        out, dres_one, dnum, dden, part, d_total, one_own, one_other, two_own, *two_other = rows_call(
            sc, tokens, q, k, v, pre, init, cos, sin, table, w_out, w_up, w_down, norm_gains, norm_biases, cotangent, block
        )
        one_got = swap_core(one_other)
        d_init = swap_core(d_total)
        two_got = [swap_core(x) for x in two_other]
        along = (swap_near, swap_far, swap_first, swap_second) if direct else (swap_first, swap_second)
        one = step([one_own, one_got], along[0])
        two_keep, two_send = small_call(
            add_cut_parts_kernel, [two_own, *two_got], [HALF, HALF], "add_cut", deps=(one[0],)
        )
        two = [two_keep, swap_first(two_send)]
        att = functools.partial(
            attend_back, sc, tokens, q, k, v, dnum, dden, pre, init, part, d_init, cos, sin, table, table_t, block
        )
        d_other, *three_other = att(deps=(two_keep,))
        three_got = [swap_core(x) for x in three_other]
        one = step(one, along[1], deps=(d_other,))
        two = step(two, swap_second, deps=(one[0],))
        d_own, three_keep, three_send = att(three_got, deps=(two[0],))
        three = [three_keep, swap_first(three_send)]
        if direct:
            one = step(one, swap_first, deps=(three_keep,))
            two = step(two, swap_near, deps=(one[0],))
            one = step(one, swap_second, deps=(two[0],))
            three = step(three, swap_second, deps=(one[0],))
            two = step(two, swap_far, deps=(three[0],))
            one = share_z(one, deps=(two[0],))
            three = cut_z(*three, deps=(one[0],))
            two = share_z(two, deps=(three[0],), neighbours=True)
            one = spread(one, deps=(two[0],))
            three = share_z(three, deps=(one[0],))
            two = spread(two, deps=(three[0],))
        else:
            three = step(three, swap_second)
            one, two, three = spread([sum_z(*one)]), spread([sum_z(*two)]), [sum_z(*three)]
        d_tokens = token_grad(sc, dres_one, d_other, d_own, w_query, w_key, w_value, deps=(two[0],))
        three = spread(three, deps=(d_tokens,))
        grad_down = gather_units(sc, one, block, True, deps=(three[0],))
        grad_up, grad_out, grad_gains, grad_biases = gather_two(sc, two, block, deps=(grad_down,))
        grad_qkv = gather_qkv(sc, three, block, deps=(grad_out,))
        return out, d_tokens, *grad_qkv, grad_out, grad_up, grad_down, grad_gains, grad_biases

    return local


def solution(mesh):
    rows, same = P(("dp", "head"), None), P()
    return jax.shard_map(
        make_local(mesh.shape["dp"], mesh.shape["head"]),
        mesh=mesh,
        in_specs=(rows,) + (same,) * 8 + (rows,),
        out_specs=(rows, rows) + (same,) * 8,
        check_vma=False,
    )
```

```python
import functools
import math

import jax
import jax.numpy as jnp
import numpy as np
from jax import lax
from jax.experimental import pallas as pl
from jax.experimental.pallas import tpu as pltpu
from jax.sharding import PartitionSpec as P

D = 768
E = 64
FF = 3072
LENGTH = 2048
CHUNK = 256
PAIR = 2 * E
PAIRS = D // PAIR
FEAT = 2 * PAIR
EPSILON = 1e-05
STEP_ANGLE = 0.5 * math.pi / LENGTH
HALF = D // 2
QUARTER = D // 4
LIMIT = 63 * 2**20
PACE = 1.0
WEIGHTS = dict(
    project=11, rows=60, attend_back=19, token_grad=10, gather_units=8, gather_qkv=5.5, gather_two=12, add_cut=2.5, add_all=2, join=2
)

f32 = jnp.float32
bf16 = jnp.bfloat16


def nn(a, b):
    return jnp.dot(a, b, preferred_element_type=f32)


def tn(a, b):
    return lax.dot_general(a, b, (((0,), (0,)), ((), ())), preferred_element_type=f32)


def nt(a, b):
    return lax.dot_general(a, b, (((1,), (1,)), ((), ())), preferred_element_type=f32)


def ordered_call(
    kernel, name, grid, in_specs, out_specs, out_shape, scratch_shapes=(), scalars=0, deps=(),
):
    deps = list(deps)

    def body(*refs):
        first = scalars + len(in_specs)
        kernel(*refs[:first], *refs[first + len(deps) :])

    call = pl.pallas_call(
        body,
        grid_spec=pltpu.PrefetchScalarGridSpec(
            num_scalar_prefetch=scalars,
            grid=grid,
            in_specs=list(in_specs) + [pl.BlockSpec(memory_space=pl.ANY)] * len(deps),
            out_specs=out_specs,
            scratch_shapes=list(scratch_shapes),
        ),
        out_shape=out_shape,
        compiler_params=pltpu.CompilerParams(vmem_limit_bytes=LIMIT),
        cost_estimate=pl.CostEstimate(
            flops=int(PACE * WEIGHTS[name] * 1.15e9) + 1, bytes_accessed=1, transcendentals=0
        ),
        name=name,
    )
    return lambda *args: call(*args, *deps)


def whole(*shape):
    return pl.BlockSpec(shape, lambda *_: (0,) * len(shape))


def by_chunk(width, last=None):
    if last is None:
        return pl.BlockSpec((CHUNK, width), lambda i, *_: (i, 0))
    return pl.BlockSpec((CHUNK, width), lambda i, *_: (last - i, 0))


ANY = pl.BlockSpec(memory_space=pl.ANY)


def softplus(x):
    return jnp.maximum(x, 0.0) + jnp.log1p(jnp.exp(-jnp.abs(x)))


def lane_head(rows):
    return (lax.broadcasted_iota(jnp.int32, (rows, PAIR), 1) >= E).astype(jnp.int32)


def row_head():
    return (lax.broadcasted_iota(jnp.int32, (FEAT, PAIR), 0) % PAIR >= E).astype(jnp.int32)


def unpack_state(packed):
    same = row_head() == lane_head(FEAT)
    left = jnp.where(same, packed, 0.0)
    right = jnp.where(same, pltpu.roll(packed, E, 1), 0.0)
    return jnp.concatenate([left, right], axis=1).astype(bf16)


def features(x, cosine, sine):
    return jnp.concatenate([x * cosine, x * sine], axis=1).astype(bf16)


def with_ones(v):
    return jnp.concatenate([v, jnp.ones_like(v)], axis=1)


def heads_apart(x, second):
    zero = jnp.zeros_like(x)
    return jnp.concatenate([jnp.where(second, zero, x), jnp.where(second, x, zero)], axis=0)


def turn_state(state, angle, on):
    cosine, sine = math.cos(angle) * on, math.sin(angle) * on
    first, second = state[:PAIR], state[PAIR:]
    return jnp.concatenate([cosine * first + sine * second, cosine * second - sine * first], axis=0)


def project_kernel(tok, wq, wk, wv, cos, sin, q_ref, k_ref, v_ref, pre_ref, tot_ref):
    @pl.when(pl.program_id(0) == 0)
    def _():
        tot_ref[...] = jnp.zeros_like(tot_ref)

    x = tok[...]
    q_ref[...] = softplus(nn(x, wq[...])).astype(bf16)
    k = softplus(nn(x, wk[...])).astype(bf16)
    k_ref[...] = k
    v = nn(x, wv[...]).astype(bf16)
    v_ref[...] = v
    same = row_head() == lane_head(FEAT)
    for p in range(PAIRS):
        cols = slice(p * PAIR, (p + 1) * PAIR)
        k_feat = features(k[:, cols].astype(f32), cos[...], sin[...])
        both = tn(k_feat, with_ones(v[:, cols]))
        pre_ref[0, p] = tot_ref[p]
        tot_ref[p] += jnp.where(same, both[:, :PAIR], both[:, PAIR:])


def project(tokens, wq, wk, wv, cos, sin):
    rows = tokens.shape[0]
    steps = rows // CHUNK
    act = jax.ShapeDtypeStruct((rows, D), bf16)
    return ordered_call(
        project_kernel,
        "project",
        grid=(steps,),
        in_specs=[by_chunk(D), whole(D, D), whole(D, D), whole(D, D), by_chunk(PAIR), by_chunk(PAIR)],
        out_specs=[
            by_chunk(D), by_chunk(D), by_chunk(D),
            pl.BlockSpec((1, PAIRS, FEAT, PAIR), lambda i: (i, 0, 0, 0)), whole(PAIRS, FEAT, PAIR),
        ],
        out_shape=[
            act, act, act,
            jax.ShapeDtypeStruct((steps, PAIRS, FEAT, PAIR), f32), jax.ShapeDtypeStruct((PAIRS, FEAT, PAIR), f32),
        ],
    )(tokens, wq, wk, wv, cos, sin)


def norm_parts(z):
    centred = z - jnp.mean(z, axis=-1, keepdims=True)
    rstd = lax.rsqrt(jnp.mean(centred * centred, axis=-1, keepdims=True) + EPSILON)
    return centred * rstd, rstd


def norm_back(t, n, rstd):
    return (t - jnp.mean(t, axis=-1, keepdims=True) - n * jnp.mean(t * n, axis=-1, keepdims=True)) * rstd


def rows_kernel(
    angle, block, sc, tok, q_ref, k_ref, v_ref, pre, init, cos, sin, table, w_out, w_up_hbm, w_down_hbm, gains, biases, cot,
    out_ref, dres_one_ref, dnum_ref, dden_ref, part_ref, tot_ref, one_own, one_other, two_own, two_first, two_second, two_rest,
    w_up, w_down, mixed, hid, slope, dhid, acc_down, acc_up, acc_out, ng, stage, norm_stage, sems, norm_sems, w_sems,
):
    core = sc[0]
    step = pl.program_id(0)
    first = step == 0

    def weight_copies():
        return (
            pltpu.make_async_copy(w_up_hbm, w_up, w_sems.at[0]),
            pltpu.make_async_copy(w_down_hbm, w_down, w_sems.at[1]),
        )

    @pl.when(first)
    def _():
        for copy in weight_copies():
            copy.start()
        ng[...] = jnp.zeros_like(ng)
        tot_ref[...] = jnp.zeros_like(tot_ref)

    later = core.astype(f32)
    second = lane_head(CHUNK) == 1
    second2 = jnp.concatenate([second, second], axis=1)
    inverse = []
    for p in range(PAIRS):
        cols = slice(p * PAIR, (p + 1) * PAIR)
        state = unpack_state(pre[0, p] + turn_state(init[p], angle, later))
        q, k, v = q_ref[:, cols], k_ref[:, cols], v_ref[:, cols]
        total = nn(features(q.astype(f32), cos[...], sin[...]), state)
        scores = (nt(q, heads_apart(k, second)) * table[...]).astype(bf16)
        total += nn(scores, heads_apart(with_ones(v), second2))
        inv = 1.0 / total[:, PAIR:]
        inverse.append(inv)
        mixed[:, cols] = (total[:, :PAIR] * inv).astype(bf16)
    z = tok[...].astype(f32) + nn(mixed[...], w_out[...])
    n0, rstd0 = norm_parts(z)
    normed = n0 * gains[0:1] + biases[0:1]
    low = normed.astype(bf16)

    @pl.when(first)
    def _():
        for copy in weight_copies():
            copy.wait()

    for j in range(FF // D):
        cols = slice(j * D, (j + 1) * D)
        h = nn(low, w_up[:, cols])
        phi = 0.5 * (1.0 + lax.erf(h * (0.5**0.5)))
        hid[:, cols] = (h * phi).astype(bf16)
        slope[:, cols] = (phi + h * jnp.exp(-0.5 * h * h) * ((2 * math.pi) ** -0.5)).astype(bf16)
    z = normed + nn(hid[...], w_down[...])
    n1, rstd1 = norm_parts(z)
    out_ref[...] = (n1 * gains[1:2] + biases[1:2]).astype(bf16)
    g = cot[...].astype(f32)
    ng[2:3] += jnp.sum(g * n1, axis=0, keepdims=True)
    ng[3:4] += jnp.sum(g, axis=0, keepdims=True)
    dres = norm_back(g * gains[1:2], n1, rstd1)
    dffn = dres.astype(bf16)
    for j in range(FF // D):
        cols = slice(j * D, (j + 1) * D)
        dhid[:, cols] = (nt(dffn, w_down[cols, :]) * slope[:, cols].astype(f32)).astype(bf16)
    g = dres + nt(dhid[...], w_up[...])
    ng[0:1] += jnp.sum(g * n0, axis=0, keepdims=True)
    ng[1:2] += jnp.sum(g, axis=0, keepdims=True)
    dres_one = norm_back(g * gains[0:1], n0, rstd0)
    dres_one_ref[...] = dres_one
    dbranch = dres_one.astype(bf16)
    dmixed = nt(dbranch, w_out[...]).astype(bf16).astype(f32)
    lane = lax.broadcasted_iota(jnp.int32, (CHUNK, PAIR), 1)
    same = row_head() == lane_head(FEAT)
    for p in range(PAIRS):
        cols = slice(p * PAIR, (p + 1) * PAIR)
        dnum = (dmixed[:, cols] * inverse[p]).astype(bf16)
        dnum_ref[:, cols] = dnum
        moment = dnum.astype(f32) * mixed[:, cols].astype(f32)
        first_sum = jnp.sum(jnp.where(second, 0.0, moment), axis=1, keepdims=True)
        second_sum = jnp.sum(jnp.where(second, moment, 0.0), axis=1, keepdims=True)
        dden = jnp.where(second, second_sum, first_sum) * (-2.0 / E)
        high = dden.astype(bf16)
        rest = (dden - high.astype(f32)).astype(bf16)
        dden = jnp.where(lane % E < E // 2, high, rest)
        dden_ref[:, cols] = dden
        both = tn(features(q_ref[:, cols].astype(f32), cos[...], sin[...]), jnp.concatenate([dnum, dden], axis=1))
        part = jnp.where(same, both[:, :PAIR], pltpu.roll(both[:, PAIR:], E, 1))
        part_ref[0, p] = part
        tot_ref[p] += part
    for j in range(FF // D):
        cols = slice(j * D, (j + 1) * D)
        acc_down[cols, :] = jnp.where(first, 0.0, acc_down[cols, :]) + tn(hid[:, cols], dffn)
        acc_up[:, cols] = jnp.where(first, 0.0, acc_up[:, cols]) + tn(low, dhid[:, cols])
    acc_out[...] = jnp.where(first, 0.0, acc_out[...]) + tn(mixed[...], dbranch)

    @pl.when(step == pl.num_programs(0) - 1)
    def _():
        slots = stage.shape[0]
        jobs = []
        for j in range(4):
            jobs.append((acc_down.at[j * D : (j + 1) * D, :], j // 2, one_own, one_other, j % 2 * D, j % 2 * D, D))
        for j in range(4):
            jobs.append((acc_up.at[:, j * D : (j + 1) * D], j // 2, two_own, two_second if j % 2 else two_first, j % 2 * D, 0, D))
        for j in range(2):
            jobs.append((acc_out.at[:, j * HALF : (j + 1) * HALF], j, two_own, two_rest, 2 * D, 0, HALF))

        def move(i, do):
            _, owner, own, other, own_at, other_at, size = jobs[i]
            slot = i % slots

            def one(to, start):
                do(pltpu.make_async_copy(stage.at[slot, :, pl.ds(0, size)], to.at[:, pl.ds(start, size)], sems.at[slot]))

            @pl.when(core == owner)
            def _():
                one(own, own_at)

            @pl.when(core != owner)
            def _():
                one(other, other_at)

        for i, (acc, owner, _, _, _, _, size) in enumerate(jobs):
            if i >= slots:
                move(i - slots, lambda copy: copy.wait())
            me = jnp.where(core == owner, sc[3 if i < 4 else 1], sc[4 if i < 4 else 2])
            for b in range(D // block):
                to = pl.multiple_of((jnp.int32(b) ^ me) * block, block)
                stage[i % slots, pl.ds(to, block), :size] = acc[b * block : (b + 1) * block, :].astype(bf16)
            move(i, lambda copy: copy.start())
        norm_stage[...] = jnp.zeros_like(norm_stage)
        copies = []
        for i, (me, to, start) in enumerate(((sc[1], two_own, 2 * D + HALF), (sc[2], two_rest, HALF))):
            base = pl.multiple_of(me * block, block)
            rows = [ng[r : r + 1, j * PAIR : (j + 1) * PAIR] for r in range(4) for j in range(PAIRS)]
            rows.append(jnp.zeros((block - len(rows), PAIR), f32))
            norm_stage[i, pl.ds(base, block), :] = jnp.concatenate(rows, axis=0).astype(bf16)
            copy = pltpu.make_async_copy(norm_stage.at[i], to.at[:, pl.ds(start, PAIR)], norm_sems.at[i])
            copy.start()
            copies.append(copy)
        for i in range(len(jobs) - slots, len(jobs)):
            move(i, lambda copy: copy.wait())
        for copy in copies:
            copy.wait()


def rows_call(sc, tokens, q, k, v, pre, init, cos, sin, table, w_out, w_up, w_down, gains, biases, cot, block):
    rows = tokens.shape[0]
    steps = rows // CHUNK

    def make(width, dtype=bf16, height=rows):
        return jax.ShapeDtypeStruct((height, width), dtype)

    def once(*shape):
        return pl.BlockSpec(shape, lambda *_: (0,) * len(shape), pipeline_mode=pl.Buffered(1))

    chunk, thin = by_chunk(D), by_chunk(PAIR)
    states = pl.BlockSpec((1, PAIRS, FEAT, PAIR), lambda i, sc: (i, 0, 0, 0))
    one, two = 2 * D, 2 * D + HALF + PAIR
    return ordered_call(
        functools.partial(rows_kernel, STEP_ANGLE * rows, block),
        "rows",
        scalars=1,
        grid=(steps,),
        in_specs=[
            chunk, chunk, chunk, chunk, states, once(PAIRS, FEAT, PAIR), thin, thin, once(CHUNK, 2 * CHUNK),
            once(D, D), ANY, ANY, once(2, D), once(2, D), chunk,
        ],
        out_specs=[chunk, chunk, chunk, chunk, states, whole(PAIRS, FEAT, PAIR)] + [ANY] * 6,
        out_shape=[
            make(D), make(D, f32), make(D), make(D), jax.ShapeDtypeStruct((steps, PAIRS, FEAT, PAIR), f32),
            jax.ShapeDtypeStruct((PAIRS, FEAT, PAIR), f32),
            make(one, bf16, D), make(one, bf16, D), make(two, bf16, D), make(D, bf16, D), make(D, bf16, D),
            make(HALF + PAIR, bf16, D),
        ],
        scratch_shapes=[
            pltpu.VMEM((D, FF), bf16), pltpu.VMEM((FF, D), bf16),
            pltpu.VMEM((CHUNK, D), bf16), pltpu.VMEM((CHUNK, FF), bf16), pltpu.VMEM((CHUNK, FF), bf16),
            pltpu.VMEM((CHUNK, FF), bf16), pltpu.VMEM((FF, D), f32), pltpu.VMEM((D, FF), f32), pltpu.VMEM((D, D), f32),
            pltpu.VMEM((4, D), f32), pltpu.VMEM((3, D, D), bf16), pltpu.VMEM((2, D, PAIR), bf16),
            pltpu.SemaphoreType.DMA((3,)), pltpu.SemaphoreType.DMA((2,)), pltpu.SemaphoreType.DMA((2,)),
        ],
    )(sc, tokens, q, k, v, pre, init, cos, sin, table, w_out, w_up, w_down, gains, biases, cot)


def sigmoid_of(soft):
    return jnp.where(soft < 0.01, soft * (1.0 - 0.5 * soft), 1.0 - jnp.exp(-soft))


def attend_back_kernel(
    angle, block, own, sc, tok, q_ref, k_ref, v_ref, dnum_ref, dden_ref, pre, init, part, d_init, cos, sin, table, table_t,
    *refs,
):
    if own:
        *got, out_ref, keep_ref, send_ref, run, acc, wide = refs
    else:
        out_ref, *other_refs, run, acc = refs
    pairs = PAIRS // 2
    later = sc[0].astype(f32)

    @pl.when(pl.program_id(0) == 0)
    def _():
        for p in range(pairs):
            run[p] = turn_state(d_init[p], -angle, 1.0 - later)

    second = lane_head(CHUNK) == 1
    second2 = jnp.concatenate([second, second], axis=1)

    for p in range(pairs):
        cols = slice(p * PAIR, (p + 1) * PAIR)
        q, k, v = q_ref[:, cols], k_ref[:, cols], v_ref[:, cols]
        q_wide, k_wide = q.astype(f32), k.astype(f32)
        dnum = dnum_ref[:, cols]
        grad = jnp.concatenate([dnum, dden_ref[:, cols]], axis=1)
        v_ones = with_ones(v)
        state = unpack_state(pre[0, p] + turn_state(init[p], angle, later))
        d_state = unpack_state(run[p])
        run[p] += part[0, p]
        dq_feat = nt(grad, state)
        dk_feat = nt(v_ones, d_state)
        dv = nn(features(k_wide, cos[...], sin[...]), d_state[:, :PAIR])
        dq = dq_feat[:, :PAIR] * cos[...] + dq_feat[:, PAIR:] * sin[...]
        dk = dk_feat[:, :PAIR] * cos[...] + dk_feat[:, PAIR:] * sin[...]
        q_apart, k_apart = heads_apart(q, second), heads_apart(k, second)
        d_scores = (nt(grad, heads_apart(v_ones, second2)) * table[...]).astype(bf16)
        dq += nn(d_scores, k_apart)
        scores_t = (nt(k, q_apart) * table_t[...]).astype(bf16)
        d_scores_t = (nt(v_ones, heads_apart(grad, second2)) * table_t[...]).astype(bf16)
        dk += nn(d_scores_t, q_apart)
        dv += nn(scores_t, heads_apart(dnum, second))
        out_ref[:, cols] = (dq.astype(bf16).astype(f32) * sigmoid_of(q_wide)).astype(bf16)
        out_ref[:, slice(HALF + p * PAIR, HALF + (p + 1) * PAIR)] = (
            dk.astype(bf16).astype(f32) * sigmoid_of(k_wide)
        ).astype(bf16)
        out_ref[:, slice(D + p * PAIR, D + (p + 1) * PAIR)] = dv.astype(bf16)
    acc[...] = jnp.where(pl.program_id(0) == 0, 0.0, acc[...]) + tn(tok[...], out_ref[...])

    @pl.when(pl.program_id(0) == pl.num_programs(0) - 1)
    def _():
        me = sc[1] if own else sc[2]
        for b in range(D // block):
            to = pl.ds(pl.multiple_of((jnp.int32(b) ^ me) * block, block), block)
            for j in range(3):
                cols = slice(j * HALF, (j + 1) * HALF)
                piece = acc[b * block : (b + 1) * block, cols]
                if own:
                    wide[to, cols] = (piece + got[j][to, :].astype(f32)).astype(bf16)
                else:
                    other_refs[j][to, :] = piece.astype(bf16)
        if own:
            keep_ref[...] = wide[:HALF]
            send_ref[...] = wide[HALF:]


def attend_back(
    sc, tokens, q, k, v, dnum, dden, pre, init, part, d_init, cos, sin, table, table_t, block, got=None, deps=()
):
    own = got is not None
    rows = q.shape[0]
    steps = rows // CHUNK
    last = steps - 1
    pairs = PAIRS // 2

    def half(sc):
        return sc[0] if own else 1 - sc[0]

    def make(height):
        return jax.ShapeDtypeStruct((height, 3 * HALF), bf16)

    chunk = pl.BlockSpec((CHUNK, HALF), lambda i, sc: (last - i, half(sc)))
    states = pl.BlockSpec((1, pairs, FEAT, PAIR), lambda i, sc: (last - i, half(sc), 0, 0))
    state = pl.BlockSpec((pairs, FEAT, PAIR), lambda i, sc: (half(sc), 0, 0))
    thin = by_chunk(PAIR, last)
    return ordered_call(
        functools.partial(attend_back_kernel, STEP_ANGLE * rows, block, own),
        "attend_back",
        scalars=1,
        deps=deps,
        grid=(steps,),
        in_specs=[
            by_chunk(D, last), chunk, chunk, chunk, chunk, chunk, states, state, states, state, thin, thin,
            whole(CHUNK, 2 * CHUNK), whole(CHUNK, 2 * CHUNK),
        ] + [whole(D, HALF)] * (3 * own),
        out_specs=[by_chunk(3 * HALF, last)] + ([whole(HALF, 3 * HALF)] * 2 if own else [whole(D, HALF)] * 3),
        out_shape=[make(rows)] + ([make(HALF)] * 2 if own else [jax.ShapeDtypeStruct((D, HALF), bf16)] * 3),
        scratch_shapes=[pltpu.VMEM((pairs, FEAT, PAIR), f32), pltpu.VMEM((D, 3 * HALF), f32)]
        + [pltpu.VMEM((D, 3 * HALF), bf16)] * own,
    )(sc, tokens, q, k, v, dnum, dden, pre, init, part, d_init, cos, sin, table, table_t, *(got or ()))


def token_grad_kernel(sc, dres_one, first, second, wq1, wk1, wv1, wq2, wk2, wv2, out):
    total = dres_one[...]
    for d, weights in ((first, (wq1, wk1, wv1)), (second, (wq2, wk2, wv2))):
        for j, w in enumerate(weights):
            total += nt(d[:, j * HALF : (j + 1) * HALF], w[...])
    out[...] = total


def token_grad(sc, dres_one, other, own, wq, wk, wv, deps=()):
    rows = own.shape[0]
    w_other = pl.BlockSpec((D, HALF), lambda i, sc: (0, 1 - sc[0]))
    w_own = pl.BlockSpec((D, HALF), lambda i, sc: (0, sc[0]))
    return ordered_call(
        token_grad_kernel,
        "token_grad",
        scalars=1,
        deps=deps,
        grid=(rows // CHUNK,),
        in_specs=[by_chunk(D), by_chunk(3 * HALF), by_chunk(3 * HALF)] + [w_other] * 3 + [w_own] * 3,
        out_specs=by_chunk(D),
        out_shape=jax.ShapeDtypeStruct((rows, D), f32),
    )(sc, dres_one, other, own, wq, wk, wv, wq, wk, wv)


def small_call(kernel, ins, out_rows, name, deps=()):
    width = ins[0].shape[1]
    many = isinstance(out_rows, (list, tuple))
    cuts = 2 if ins[0].shape[0] == D and all(x.shape == ins[0].shape for x in ins) else 1

    def spec(x_rows, x_width):
        return pl.BlockSpec((x_rows, x_width // cuts), lambda i: (0, i))

    def shape(rows):
        return jax.ShapeDtypeStruct((rows, width), bf16)

    return ordered_call(
        kernel,
        name,
        deps=deps,
        grid=(cuts,),
        in_specs=[spec(*x.shape) for x in ins],
        out_specs=[spec(r, width) for r in out_rows] if many else spec(out_rows, width),
        out_shape=[shape(r) for r in out_rows] if many else shape(out_rows),
    )(*ins)


def add_cut_kernel(a, b, *outs):
    rows = outs[0].shape[0]
    for i, out in enumerate(outs):
        at = slice(i * rows, (i + 1) * rows)
        out[...] = (a[at].astype(f32) + b[at].astype(f32)).astype(bf16)


def add_cut_parts_kernel(a, first, second, rest, keep, send):
    start = 0
    for part in (first, second, rest):
        cols = slice(start, start + part.shape[1])
        keep[:, cols] = (a[:HALF, cols].astype(f32) + part[:HALF].astype(f32)).astype(bf16)
        send[:, cols] = (a[HALF:, cols].astype(f32) + part[HALF:].astype(f32)).astype(bf16)
        start += part.shape[1]


def add_all_kernel(*refs):
    total = refs[0][...].astype(f32)
    for ref in refs[1:-1]:
        total += ref[...].astype(f32)
    refs[-1][...] = total.astype(bf16)


def join_kernel(*refs):
    rows = refs[0].shape[0]
    for i, ref in enumerate(refs[:-1]):
        refs[-1][i * rows : (i + 1) * rows] = ref[...]


def add_cut(a, b, parts, deps=()):
    return small_call(add_cut_kernel, [a, b], [a.shape[0] // parts] * parts, "add_cut", deps)


def add_all(parts, deps=()):
    return small_call(add_all_kernel, parts, parts[0].shape[0], "add_all", deps)


def join(parts, deps=()):
    return small_call(join_kernel, parts, len(parts) * parts[0].shape[0], "join", deps)


def restore(me, block, quarters, put, along_z=False):
    count = QUARTER // block
    for i, ref in enumerate(quarters):
        for j in range(count):
            place = j * len(quarters) + i if along_z else i * count + j
            put(
                pl.multiple_of((jnp.int32(place) ^ me) * block, block),
                ref[j * block : (j + 1) * block, :].astype(f32),
            )


def gather_kernel(block, by_rows, sc, *refs):
    mine, other, out = refs[:4], refs[4:8], refs[8]
    own_me, other_me = (sc[3], sc[4]) if by_rows else (sc[1], sc[2])

    def put(row, piece):
        out[pl.ds(row, block), :] = piece

    is_mine = pl.program_id(0) // 2 == sc[0]

    @pl.when(is_mine)
    def _():
        restore(own_me, block, mine, put, by_rows)

    @pl.when(jnp.logical_not(is_mine))
    def _():
        restore(other_me, block, other, put, by_rows)


def gather_units(sc, parts, block, by_rows, deps=()):
    def at(own):
        def index(g, sc):
            return (0, jnp.clip(g - 2 * (sc[0] if own else 1 - sc[0]), 0, 1))

        return pl.BlockSpec((QUARTER, D), index)

    return ordered_call(
        functools.partial(gather_kernel, block, by_rows),
        "gather_units",
        scalars=1,
        deps=deps,
        grid=(4,),
        in_specs=[at(True)] * 4 + [at(False)] * 4,
        out_specs=pl.BlockSpec((D, D), (lambda g, sc: (g, 0)) if by_rows else (lambda g, sc: (0, g))),
        out_shape=jax.ShapeDtypeStruct((4 * D, D) if by_rows else (D, 4 * D), f32),
    )(sc, *parts)


def half_of(block, sc, group, start, size, store):
    mine, other = group[:4], group[4:]

    def cut(refs):
        return [ref.at[:, start : start + size] for ref in refs]

    is_mine = pl.program_id(0) == sc[0]

    @pl.when(is_mine)
    def _():
        restore(sc[1], block, cut(mine), store)

    @pl.when(jnp.logical_not(is_mine))
    def _():
        restore(sc[2], block, cut(other), store)


def gather_qkv_kernel(block, sc, *refs):
    for j, out in enumerate(refs[8:]):
        def put(row, piece, out=out):
            out[pl.ds(row, block), :] = piece

        half_of(block, sc, refs[:8], j * HALF, HALF, put)


def gather_qkv(sc, parts, block, deps=()):
    shape = jax.ShapeDtypeStruct((D, D), f32)
    return ordered_call(
        functools.partial(gather_qkv_kernel, block),
        "gather_qkv",
        scalars=1,
        deps=deps,
        grid=(2,),
        in_specs=[whole(QUARTER, 3 * HALF)] * 8,
        out_specs=[pl.BlockSpec((D, HALF), lambda g, sc: (0, g))] * 3,
        out_shape=[shape] * 3,
    )(sc, *parts)


def gather_two_kernel(block, sc, *refs):
    units, group = (*refs[:8], refs[16]), refs[8:16]
    out, gains, biases, rows = refs[17:]
    step = pl.program_id(0)
    gather_kernel(block, False, sc, *units)

    def put(row, piece):
        out[pl.ds(row, block), :] = piece

    def put_norm(row, piece):
        rows[pl.ds(row, block), :] = piece

    @pl.when(step < 2)
    def _():
        half_of(block, sc, group, 0, HALF, put)

    @pl.when(step == 0)
    def _():
        half_of(block, sc, group, HALF, PAIR, put_norm)
        for i in range(2):
            for j in range(PAIRS):
                cols = slice(j * PAIR, (j + 1) * PAIR)
                first, second = 2 * i * PAIRS + j, (2 * i + 1) * PAIRS + j
                gains[i : i + 1, cols] = rows[first : first + 1, :]
                biases[i : i + 1, cols] = rows[second : second + 1, :]


def gather_two(sc, parts, block, deps=()):
    def at(own):
        def index(g, sc):
            return (0, jnp.clip(g - 2 * (sc[0] if own else 1 - sc[0]), 0, 1))

        return pl.BlockSpec((QUARTER, D), index)

    norm = jax.ShapeDtypeStruct((2, D), f32)
    rest = pl.BlockSpec((QUARTER, HALF + PAIR), lambda g, sc: (0, 2 * D // (HALF + PAIR)))
    return ordered_call(
        functools.partial(gather_two_kernel, block),
        "gather_two",
        scalars=1,
        deps=deps,
        grid=(4,),
        in_specs=[at(True)] * 4 + [at(False)] * 4 + [rest] * 8,
        out_specs=[
            pl.BlockSpec((D, D), lambda g, sc: (0, g)), pl.BlockSpec((D, HALF), lambda g, sc: (0, jnp.minimum(g, 1))),
            whole(2, D), whole(2, D),
        ],
        out_shape=[jax.ShapeDtypeStruct((D, 4 * D), f32), jax.ShapeDtypeStruct((D, D), f32), norm, norm],
        scratch_shapes=[pltpu.VMEM((D, PAIR), f32)],
    )(sc, *parts, *parts)


def make_local(n_dp, n_head):
    n_z = n_dp // 2
    direct = n_z == 4
    places = 4 if direct else 1
    block = QUARTER // places
    both_axes = ("dp", "head")

    def swap(x, partner):
        pairs = []
        for d in range(n_dp):
            for h in range(n_head):
                to_d, to_h = partner(d, h)
                pairs.append((d * n_head + h, to_d * n_head + to_h))
        return lax.ppermute(x, both_axes, pairs)

    def swap_core(x):
        return swap(x, lambda d, h: (d, h ^ 1))

    def swap_first(x):
        return swap(x, lambda d, h: (d ^ 1, h) if h % 2 else (d, h ^ 2))

    def swap_second(x):
        return swap(x, lambda d, h: (d, h ^ 2) if h % 2 else (d ^ 1, h))

    def swap_z(x, k):
        return swap(x, lambda d, h: (d ^ (2 * k), h))

    def sum_z(keep, got):
        both = keep.astype(f32) + got.astype(f32)
        same_z = [[2 * i + j for i in range(n_z)] for j in range(2)]
        return lax.psum(both, "dp", axis_index_groups=same_z).astype(bf16)

    def cut_z(keep, got, deps=()):
        parts = add_cut(keep, got, 4, deps)
        return [parts[0], swap_z(parts[1], 2), swap_z(parts[2], 1), swap_z(parts[3], 3)]

    def share_z(parts, deps=(), neighbours=False):
        share = add_all(parts, deps)
        near, far = swap_z(share, 1), swap_z(share, 2)
        return [share, far, near, swap_z(far, 1) if neighbours else swap_z(share, 3)]

    def step(pair, swap_next, deps=()):
        keep, send = add_cut(*pair, 2, deps)
        return [keep, swap_next(send)]

    def swap_near(x):
        return swap_z(x, 1)

    def swap_far(x):
        return swap_z(x, 2)

    def spread(parts, deps=()):
        own = join(parts, deps) if direct else parts[0]
        second = swap_second(own)
        first = swap_first(own)
        both = swap_first(second)
        quarters = [own, second, first, both]
        return quarters + [swap_core(x) for x in quarters]

    def local(tokens, w_query, w_key, w_value, w_out, w_up, w_down, norm_gains, norm_biases, cotangent):
        rows = tokens.shape[0]
        assert LENGTH == 2 * rows and n_head % 4 == 0 and n_dp % 2 == 0
        head, dp = lax.axis_index("head"), lax.axis_index("dp")
        core, x, y, z = head % 2, head // 2, dp % 2, dp // 2
        rank = z % 2 * 2 + z // 2 if direct else 0
        by_x, by_y = (2 * x + y) * places + rank, (2 * y + x) * places + rank
        z_x, z_y = (rank * 4 + 2 * x + y, rank * 4 + 2 * y + x) if direct else (by_x, by_y)
        sc = jnp.stack([core, *(jnp.where(core == 0, *pair) for pair in ((by_x, by_y), (by_y, by_x), (z_x, z_y), (z_y, z_x)))])
        sc = sc.astype(jnp.int32)
        angle = STEP_ANGLE * np.arange(rows)
        cos = jnp.asarray(np.broadcast_to(np.cos(angle)[:, None], (rows, PAIR)), f32)
        sin = jnp.asarray(np.broadcast_to(np.sin(angle)[:, None], (rows, PAIR)), f32)
        gap = np.arange(CHUNK)[:, None] - np.arange(CHUNK)[None, :]
        weights = np.where(gap >= 0, np.cos(STEP_ANGLE * gap), 0.0)
        table, table_t = (jnp.asarray(np.concatenate([w, w], axis=1), f32) for w in (weights, weights.T))

        q, k, v, pre, total = project(tokens, w_query, w_key, w_value, cos, sin)
        init = swap_core(total)
        out, dres_one, dnum, dden, part, d_total, one_own, one_other, two_own, *two_other = rows_call(
            sc, tokens, q, k, v, pre, init, cos, sin, table, w_out, w_up, w_down, norm_gains, norm_biases, cotangent, block
        )
        one_got = swap_core(one_other)
        d_init = swap_core(d_total)
        two_got = [swap_core(x) for x in two_other]
        along = (swap_near, swap_far, swap_first, swap_second) if direct else (swap_first, swap_second)
        one = step([one_own, one_got], along[0])
        two_keep, two_send = small_call(
            add_cut_parts_kernel, [two_own, *two_got], [HALF, HALF], "add_cut", deps=(one[0],)
        )
        two = [two_keep, swap_first(two_send)]
        att = functools.partial(
            attend_back, sc, tokens, q, k, v, dnum, dden, pre, init, part, d_init, cos, sin, table, table_t, block
        )
        d_other, *three_other = att(deps=(two_keep,))
        three_got = [swap_core(x) for x in three_other]
        one = step(one, along[1], deps=(d_other,))
        two = step(two, swap_second, deps=(one[0],))
        d_own, three_keep, three_send = att(three_got, deps=(two[0],))
        three = [three_keep, swap_first(three_send)]
        if direct:
            one = step(one, swap_first, deps=(three_keep,))
            two = step(two, swap_near, deps=(one[0],))
            one = step(one, swap_second, deps=(two[0],))
            three = step(three, swap_second, deps=(one[0],))
            two = step(two, swap_far, deps=(three[0],))
            one = share_z(one, deps=(two[0],))
            three = cut_z(*three, deps=(one[0],))
            two = share_z(two, deps=(three[0],), neighbours=True)
            one = spread(one, deps=(two[0],))
            three = share_z(three, deps=(one[0],))
            two = spread(two, deps=(three[0],))
        else:
            three = step(three, swap_second)
            one, two, three = spread([sum_z(*one)]), spread([sum_z(*two)]), [sum_z(*three)]
        d_tokens = token_grad(sc, dres_one, d_other, d_own, w_query, w_key, w_value, deps=(two[0],))
        three = spread(three, deps=(d_tokens,))
        grad_down = gather_units(sc, one, block, True, deps=(three[0],))
        grad_up, grad_out, grad_gains, grad_biases = gather_two(sc, two, block, deps=(grad_down,))
        grad_qkv = gather_qkv(sc, three, block, deps=(grad_out,))
        return out, d_tokens, *grad_qkv, grad_out, grad_up, grad_down, grad_gains, grad_biases

    return local


def solution(mesh):
    rows, same = P(("dp", "head"), None), P()
    return jax.shard_map(
        make_local(mesh.shape["dp"], mesh.shape["head"]),
        mesh=mesh,
        in_specs=(rows,) + (same,) * 8 + (rows,),
        out_specs=(rows, rows) + (same,) * 8,
        check_vma=False,
    )
```
